512 devices in a mesh: grp: 2 (over z_hi), seq: 8 (over y, core), hid: 32 (over x, z_lo).
Axes of the slice: x: 4, y: 4, z: 16 (z_hi: 2, z_lo: 8; z = z_hi * 8 + z_lo), core: 2. Of those that a mesh axis runs over, the one named last changes fastest.
Arguments:
- queries: bfloat16 [64, 4, 64, 576], P(('grp', 'hid')), may hold values from -25 to 25
- new_latents: bfloat16 [64, 4, 576], P(('grp', 'hid')), may hold values from -4 to 4
- latent_cache: bfloat16 [64, 2048, 576], P(('grp', 'hid'), 'seq'), may hold values from -4 to 4
- lengths: int32 [64], P(('grp', 'hid')), may hold values from 1 to 2048, 65536 in all
- positions: int32 [64], P(('grp', 'hid')), may hold values from 0 to 32767
- value_up: bfloat16 [64, 512, 128], P(('grp', 'hid')), may hold values from -0.8984375 to 0.8984375
- output_weight: bfloat16 [8192, 8192], P(('grp', 'hid'), 'seq'), may hold values from -0.0625 to 0.0625
- residual: bfloat16 [256, 8192], P(None, 'seq'), may hold values from -64 to 64
- norm_gain: float32 [8192], P('seq'), may hold values from 0.1 to 1.9
- gate_weight: bfloat16 [8192, 16384], P('seq', ('grp', 'hid')), may hold values from -0.0625 to 0.0625
- up_weight: bfloat16 [8192, 16384], P('seq', ('grp', 'hid')), may hold values from -0.0625 to 0.0625
- down_weight: bfloat16 [16384, 8192], P(('grp', 'hid'), 'seq'), may hold values from -0.046875 to 0.046875
Outputs:
- layer_out: bfloat16 [256, 8192], P(('grp', 'hid'), 'seq')
The draws below stay inside these ranges and needn't reach their ends.
Inputs may be any that keep to these rules, and one draw needn't show every extreme that they name: `lengths`: some row holds exactly 2048 cached tokens.
All inputs are finite; a program needn't handle non-finite values. No bound on the sum of `lengths` on one device may be relied on, other than what follows from the above.
Results may differ from the reference program's by a relative error of at most 0.022.
Values may be sent and summed in bfloat16 or wider, within the bound.
A program may use at most 64 MiB of HBM per device.

```python
import math
import jax
import jax.numpy as jnp
import numpy as np
from jax import lax

D = 8192
FF = 16384
LATENT = 512
ROPE_DIM = 64
HEAD_DIM = 128
NEW_TOK = 4
HEADS = 64
ROWS = 64
CTX = 2048
TOKENS = 256


score_scale = 192.0 ** (-0.5)


def anchor_draws(key):
    anchor = jax.random.normal(jax.random.fold_in(key, 101), (ROWS, LATENT + ROPE_DIM), jnp.float32)
    fresh_anchor = jax.random.normal(jax.random.fold_in(key, 102), (ROWS, LATENT + ROPE_DIM), jnp.float32)
    return (anchor, fresh_anchor)


def signed_anchor(anchor, limit):
    return jnp.concatenate([jnp.sign(anchor[:, :LATENT]), jnp.clip(anchor[:, LATENT:], -limit, limit)], axis=1)


def draw_latent_cache(key, part):
    anchor, fresh_anchor = anchor_draws(key)
    key = jax.random.fold_in(key, 3)
    filler = jnp.clip(jax.random.normal(key, (ROWS, CTX, LATENT + ROPE_DIM), jnp.float32), -4.0, 4.0)
    leading = signed_anchor(anchor, 4.0)
    return filler.at[:, 0, :].set(leading).astype(jnp.bfloat16)


def draw_new_latents(key, part):
    anchor, fresh_anchor = anchor_draws(key)
    key = jax.random.fold_in(key, 4)
    filler = jnp.clip(jax.random.normal(key, (ROWS, NEW_TOK, LATENT + ROPE_DIM), jnp.float32), -4.0, 4.0)
    leading = signed_anchor(fresh_anchor, 4.0)
    return filler.at[:, 0, :].set(leading).astype(jnp.bfloat16)


def aligned_queries(anchor, fresh_anchor, baseline):
    cache_sign = jnp.sign(anchor[:, :LATENT])
    new_sign = jnp.sign(fresh_anchor[:, :LATENT])
    row_index = jnp.arange(ROWS)
    level = row_index // 8 % 3
    target_score = jnp.where(level == 0, 120.0, jnp.where(level == 1, 240.0, 420.0))
    strength = target_score / (score_scale * 0.5 * LATENT)
    target = strength[:, None] * 0.5 * (cache_sign + new_sign) + 2.0 / (score_scale * LATENT) * cache_sign
    aligned = jnp.concatenate([target, jnp.zeros((ROWS, ROPE_DIM), jnp.float32)], axis=1)
    chosen = (row_index % 8 == 0)[:, None, None] & (jnp.arange(HEADS) % 16 == 3)[None, None, :]
    return jnp.where(chosen[..., None], aligned[:, None, None, :], baseline)


def draw_queries(key, part):
    anchor, fresh_anchor = anchor_draws(key)
    key = jax.random.fold_in(key, 5)
    shape = (ROWS, NEW_TOK, HEADS, LATENT + ROPE_DIM)
    baseline = jnp.clip(jax.random.normal(key, shape, jnp.float32), -4.0, 4.0)
    return aligned_queries(anchor, fresh_anchor, baseline).astype(jnp.bfloat16)


def draw_residual(key, part):
    key = jax.random.fold_in(key, 7)
    column_pos = jnp.arange(D, dtype=jnp.float32) / max(D - 1, 1)
    baseline = jnp.clip(jax.random.normal(key, (TOKENS, D), jnp.float32), -4.0, 4.0)
    result = 0.5 * baseline * (3.0 ** (0.5 * column_pos))[None, :]
    return result.astype(jnp.bfloat16)


def with_ends(values, key, low, high):
    spot = [jax.random.randint(jax.random.fold_in(key, axis), (), 0, length) for axis, length in enumerate(values.shape)]
    main_axis = values.shape.index(max(values.shape))
    next_to = spot[:main_axis] + [(spot[main_axis] + 1) % values.shape[main_axis]] + spot[main_axis + 1:]
    return values.at[tuple(spot)].set(low).at[tuple(next_to)].set(high)


def levels(rng, shape, cuts, smallest, top_value):
    factor_of, own = 1.0, jax.random.fold_in(rng, 6)
    for position, parts in cuts:
        steps = jnp.exp(jax.random.uniform(jax.random.fold_in(own, position), (parts,), jnp.float32, smallest / len(cuts), top_value / len(cuts)))
        factor_of = factor_of * jnp.repeat(steps, shape[position] // parts).reshape([-1 if axis == position else 1 for axis in range(len(shape))])
    return factor_of


def split_up(amount, total, reach, slope):
    weights = [(1 << 20) // math.isqrt(standing ** slope) + 1 for standing in range(2, amount + 1)]
    spare, counts = total - reach - (amount - 1), [1] * (amount - 1)
    while spare > 0:
        free = [i for i in range(amount - 1) if counts[i] < reach]
        pool, remaining = sum([weights[i] for i in free]), spare
        for i in free:
            addition = min(reach - counts[i], max(1, remaining * weights[i] // pool), spare)
            counts[i] = counts[i] + addition
            spare = spare - addition
    return np.array([reach] + counts)


def uneven(key, count, total, most, lean):
    if count == 2:
        one = jax.random.randint(key, (), max(1, total - most), min(most, total - 1) + 1)
        return jnp.stack([one, total - one])
    sizes = jnp.asarray(split_up(count, total, most, lean), jnp.int32)
    couples = (count - 1) // 2
    giver, taker = sizes[1:1 + 2 * couples:2], sizes[2:2 + 2 * couples:2]
    margin = jnp.minimum(giver - 1, most - taker)
    moved = jax.random.randint(jax.random.fold_in(key, 1), (couples,), 0, 1 << 20) % (margin + 1)
    sizes = sizes.at[1:1 + 2 * couples:2].set(giver - moved).at[2:2 + 2 * couples:2].set(taker + moved)
    return sizes[jax.random.permutation(jax.random.fold_in(key, 2), count)]


def noise(rng, dims, width, most, shards=(), kind=jnp.bfloat16):
    drawn = width * jax.random.normal(rng, dims, jnp.float32)
    if shards:
        drawn = drawn * levels(rng, dims, shards, -0.22, 0.18)
    return jnp.clip(drawn, -most, most).astype(kind)


def setup_inputs(seed: int = 0) -> dict:
    arg_keys = jax.random.split(jax.random.key(seed), 13)
    return {
        "queries": draw_queries(jax.random.fold_in(arg_keys[12], 71), 0),
        "new_latents": draw_new_latents(jax.random.fold_in(arg_keys[12], 71), 0),
        "latent_cache": draw_latent_cache(jax.random.fold_in(arg_keys[12], 71), 0),
        "lengths": uneven(arg_keys[3], ROWS, ROWS * CTX // 2, CTX, 2).astype(jnp.int32),
        "positions": with_ends(jax.random.randint(arg_keys[4], (ROWS,), 0, 32768), jax.random.fold_in(arg_keys[4], 1), 0, 32767).astype(jnp.int32),
        "value_up": noise(arg_keys[5], (HEADS, LATENT, HEAD_DIM), 0.15, 0.8984375, ((0, 64),)),
        "output_weight": noise(arg_keys[6], (HEADS * HEAD_DIM, D), (HEADS * HEAD_DIM) ** -0.5, 0.0625, ((0, 64), (1, 8))),
        "residual": draw_residual(jax.random.fold_in(arg_keys[12], 71), 0),
        "norm_gain": jnp.clip(1.0 + 0.18 * jax.random.normal(arg_keys[8], (D,), jnp.float32), 0.1, 1.9),
        "gate_weight": noise(arg_keys[9], (D, FF), D ** -0.5, 0.0625, ((0, 8), (1, 64))),
        "up_weight": noise(arg_keys[10], (D, FF), D ** -0.5, 0.0625, ((0, 8), (1, 64))),
        "down_weight": noise(arg_keys[11], (FF, D), FF ** -0.5, 0.046875, ((0, 64), (1, 8))),
    }


score_scale = 192.0 ** (-0.5)

def rope_tables(positions, count, halfwidth):
    counter = jnp.arange(halfwidth, dtype=jnp.float32)
    frequency = jnp.exp(counter * (-math.log(1000000.0) / halfwidth))
    places = positions.astype(jnp.float32)[:, None] + jnp.arange(count, dtype=jnp.float32)[None, :]
    angles = places[:, :, None] * frequency
    return (jnp.cos(angles), jnp.sin(angles))

def rotate(vector, cosines, sines):
    halfwidth = cosines.shape[-1]
    leading = vector[..., :halfwidth]
    trailing = vector[..., halfwidth:]
    return jnp.concatenate([leading * cosines - trailing * sines, trailing * cosines + leading * sines], axis=-1)

def full_inputs(queries, new_latents, positions):
    latent_width = LATENT
    halfwidth = (queries.shape[-1] - latent_width) // 2
    cosines, sines = rope_tables(positions, queries.shape[1], halfwidth)
    query_rope = rotate(queries[..., latent_width:].astype(jnp.float32), cosines[:, :, None, :], sines[:, :, None, :])
    full_queries = jnp.concatenate([queries[..., :latent_width], query_rope.astype(jnp.bfloat16)], axis=-1)
    key_rope = rotate(new_latents[..., latent_width:].astype(jnp.float32), cosines, sines)
    new_keys = jnp.concatenate([new_latents[..., :latent_width], key_rope.astype(jnp.bfloat16)], axis=-1)
    return (full_queries, new_keys)

def attend(entries):
    query_row, key_rows, new_keys, length = entries
    query_wide = query_row.astype(jnp.float32)
    scores = jnp.einsum('thc,jc->thj', query_wide, key_rows.astype(jnp.float32)) * score_scale
    usable = (jnp.arange(CTX, dtype=jnp.int32) < length)[None, None, :]
    nearby = jnp.einsum('thc,uc->thu', query_wide, new_keys.astype(jnp.float32)) * score_scale
    causal = (jnp.arange(NEW_TOK)[None, :] <= jnp.arange(NEW_TOK)[:, None])[:, None, :]
    largest = jnp.maximum(lax.optimization_barrier(jnp.max(jnp.where(usable, scores, -1e+30), axis=-1)), lax.optimization_barrier(jnp.max(jnp.where(causal, nearby, -1e+30), axis=-1)))
    far_weights = jnp.where(usable, jnp.exp(scores - largest[..., None]), 0.0)
    near_weights = jnp.where(causal, jnp.exp(nearby - largest[..., None]), 0.0)
    totals = lax.optimization_barrier(jnp.sum(far_weights, axis=-1)) + lax.optimization_barrier(jnp.sum(near_weights, axis=-1))
    far_rounded = lax.optimization_barrier(far_weights.astype(jnp.bfloat16)).astype(jnp.float32)
    near_rounded = lax.optimization_barrier(near_weights.astype(jnp.bfloat16)).astype(jnp.float32)
    mixture = jnp.einsum('thj,jc->thc', far_rounded, key_rows[:, :LATENT].astype(jnp.float32))
    mixture = mixture + jnp.einsum('thu,uc->thc', near_rounded, new_keys[:, :LATENT].astype(jnp.float32))
    return (mixture / totals[..., None]).astype(jnp.bfloat16)

def reference(queries, new_latents, latent_cache, lengths, positions, value_up, output_weight, residual, norm_gain, gate_weight, up_weight, down_weight):
    full_queries, new_keys = full_inputs(queries, new_latents, positions)
    head_out = lax.map(attend, (full_queries, latent_cache, new_keys, lengths.astype(jnp.int32)))
    values = jnp.einsum('rthc,hcv->rthv', head_out.astype(jnp.float32), value_up.astype(jnp.float32))
    values = values.astype(jnp.bfloat16).reshape(TOKENS, HEADS * HEAD_DIM)
    stream = residual.astype(jnp.float32) + jnp.dot(values, output_weight, preferred_element_type=jnp.float32)
    scaled = (stream * norm_gain).astype(jnp.bfloat16)
    inverse_rms = lax.rsqrt(lax.optimization_barrier(jnp.mean(stream * stream, axis=1, keepdims=True)) + 1e-06)
    gate_act = jnp.dot(scaled, gate_weight, preferred_element_type=jnp.float32) * inverse_rms
    up_act = jnp.dot(scaled, up_weight, preferred_element_type=jnp.float32) * inverse_rms
    hidden = (jax.nn.silu(gate_act) * up_act).astype(jnp.bfloat16)
    return (stream + jnp.dot(hidden, down_weight, preferred_element_type=jnp.float32)).astype(jnp.bfloat16)
```

```python
import functools
import math

import jax
import jax.numpy as jnp
from jax import lax
from jax.experimental import pallas as pl
from jax.experimental.pallas import tpu as pltpu
from jax.sharding import PartitionSpec as P

D = 8192
LATENT = 512
ROPE = 64
NX, NZ, NS = 4, 16, 8
MESH = pl.DeviceIdType.MESH
BF = jnp.bfloat16
F32 = jnp.float32
score_scale = 192.0 ** (-0.5)


def rope_tables(positions, count, halfwidth):
    counter = jnp.arange(halfwidth, dtype=F32)
    frequency = jnp.exp(counter * (-math.log(1000000.0) / halfwidth))
    places = positions.astype(F32)[:, None] + jnp.arange(count, dtype=F32)[None, :]
    angles = places[:, :, None] * frequency
    return (jnp.cos(angles), jnp.sin(angles))


def rotate(vector, cosines, sines):
    halfwidth = cosines.shape[-1]
    leading = vector[..., :halfwidth]
    trailing = vector[..., halfwidth:]
    return jnp.concatenate(
        [leading * cosines - trailing * sines, trailing * cosines + leading * sines], axis=-1
    )


def dot(a, b):
    return lax.dot_general(a, b, (((1,), (0,)), ((), ())), preferred_element_type=F32)


def dot_t(a, b):
    return lax.dot_general(a, b, (((1,), (1,)), ((), ())), preferred_element_type=F32)


def iota(shape, axis):
    return lax.broadcasted_iota(jnp.int32, shape, axis)


def one_hot(rows, cols, source_of):
    return jnp.where(iota((rows, cols), 1) == source_of(iota((rows, cols), 0)), 1.0, 0.0).astype(BF)


def remote(src, dst, send_sem, recv_sem, device):
    return pltpu.make_async_remote_copy(
        src_ref=src, dst_ref=dst, send_sem=send_sem, recv_sem=recv_sem,
        device_id=device, device_id_type=MESH,
    )


def wait_bytes(ref, sem):
    pltpu.make_async_copy(ref, ref, sem).wait()


def kernel(
    len_ref, tab_ref, newk_ref, gain_ref,
    q_hbm, k_hbm, vup_hbm, wo_hbm, res_hbm, wg_hbm, wu_hbm, wd_hbm,
    out_ref,
    q, k, vup, wo, res, wg, wu, wd,
    asend, arecv, xs, xr, zs, zr, vbuf,
    os_, orx, oz, orz, st, agb, gs, gr, hb, ds_, drx, dz, drz,
    lsem, ssem, rsem, vssem, vrsem,
):
    grp, seq, hid = lax.axis_index("grp"), lax.axis_index("seq"), lax.axis_index("hid")
    x, z = hid // 8, grp * 8 + hid % 8
    y, core = seq // 2, seq % 2

    def at(xx, zz, ss):
        return (zz // 8, ss, xx * 8 + zz % 8)

    def each(count, me, fn):
        def step(i, carry):
            fn((me + i) % count)
            return carry
        lax.fori_loop(1, count, step, 0)

    def x_peers(fn):
        each(NX, x, lambda p: fn(p, at(p, z, seq)))

    def z_peers(fn):
        each(NZ, z, lambda p: fn(p, at(x, p, seq)))

    def s_peers(fn):
        each(NS, seq, lambda p: fn(p, at(x, z, p)))

    loads = [
        pltpu.make_async_copy(a, b, lsem.at[i])
        for i, (a, b) in enumerate([
            (q_hbm, q), (k_hbm, k), (vup_hbm, vup), (wo_hbm, wo), (res_hbm, res),
            (wg_hbm, wg), (wu_hbm, wu), (wd_hbm, wd),
        ])
    ]
    for load in loads:
        load.start()

    barrier = pltpu.get_barrier_semaphore()

    def greet(p, device):
        pl.semaphore_signal(barrier, inc=1, device_id=device, device_id_type=MESH)

    x_peers(greet)
    z_peers(greet)
    s_peers(greet)

    loads[0].wait()
    loads[1].wait()
    rope_in = q[:, LATENT:]
    turn_r, turn_c = iota((ROPE, ROPE), 0), iota((ROPE, ROPE), 1)
    turn = jnp.where(
        turn_c == turn_r + 32, 1.0, jnp.where(turn_c == turn_r - 32, -1.0, 0.0)
    ).astype(BF)
    turned = dot(rope_in, turn)
    cosines = jnp.concatenate([jnp.broadcast_to(tab_ref[t:t + 1, :], (64, ROPE)) for t in range(4)], axis=0)
    sines = jnp.concatenate([jnp.broadcast_to(tab_ref[t + 4:t + 5, :], (64, ROPE)) for t in range(4)], axis=0)
    q_rope = (rope_in.astype(F32) * cosines + turned * sines).astype(BF)
    q_lat = q[:, :LATENT]
    far = (dot_t(q_lat, k[:, :LATENT]) + dot_t(q_rope, k[:, LATENT:])) * score_scale
    near = (dot_t(q_lat, newk_ref[:, :LATENT]) + dot_t(q_rope, newk_ref[:, LATENT:])) * score_scale
    usable = iota((256, 256), 1) + seq * 256 < len_ref[0]
    causal = iota((256, 16), 1) + seq * 1024 <= iota((256, 16), 0) // 64
    peak = jnp.maximum(
        jnp.max(jnp.where(usable, far, -1e30), axis=1, keepdims=True),
        jnp.max(jnp.where(causal, near, -1e30), axis=1, keepdims=True),
    )
    peak = jnp.floor(peak * (1.0 / 32.0)) * 32.0
    far_w = jnp.where(usable, jnp.exp(far - peak), 0.0)
    near_w = jnp.where(causal, jnp.exp(near - peak), 0.0)
    total = jnp.sum(far_w, axis=1, keepdims=True) + jnp.sum(near_w, axis=1, keepdims=True)
    mixture = dot(far_w.astype(BF), k[:, :LATENT]) + dot(near_w.astype(BF), newk_ref[:, :LATENT])
    asend[:, :LATENT] = mixture.astype(BF)
    lane = iota((256, 128), 1)
    high = total.astype(BF).astype(F32)
    asend[:, LATENT:] = jnp.where(
        lane == 0, peak, jnp.where(lane == 1, high, total - high)
    ).astype(BF)

    pl.semaphore_wait(barrier, (NX - 1) + (NZ - 1) + (NS - 1))

    def rows32(i):
        return pl.ds(pl.multiple_of(i * 32, 32), 32)

    s_peers(lambda p, device: remote(
        asend.at[rows32(p)], arecv.at[seq], ssem.at[0], rsem.at[0], device).start())
    arecv[seq] = asend[rows32(seq)]
    perm_one = one_hot(128, 128, lambda o: (o % 4) * 32 + o // 4)
    perm_two = one_hot(128, 128, lambda o: (o // 4 % 4) * 32 + (o // 16) * 4 + o % 4)
    wait_bytes(arecv.at[0:NS - 1], rsem.at[0])

    aux = [arecv[i, :, LATENT:].astype(F32) for i in range(NS)]
    top = functools.reduce(jnp.maximum, [a[:, 0:1] for a in aux])
    factors = [jnp.exp(a[:, 0:1] - top) for a in aux]
    totals = sum(f * (a[:, 1:2] + a[:, 2:3]) for f, a in zip(factors, aux))
    mixed = sum(f * arecv[i, :, :LATENT].astype(F32) for i, f in enumerate(factors))
    heads = (mixed / totals).astype(BF)

    stacked = jnp.concatenate([heads[:, 128 * i:128 * i + 128] for i in range(4)], axis=0)
    xs[...] = dot(perm_one, stacked).astype(BF).reshape(NX, 32, 128)
    x_peers(lambda p, device: remote(
        xs.at[p], xr.at[x], ssem.at[1], rsem.at[1], device).start())
    xr[x] = xs[x]
    wait_bytes(xr.at[0:NX - 1], rsem.at[1])
    zs[...] = dot(perm_two, xr[...].reshape(128, 128)).astype(BF).reshape(8, 16, 128)

    def to_head(j, carry):
        p = core * 8 + j

        @pl.when(p != z)
        def _():
            remote(zs.at[j], zr.at[z], ssem.at[2], rsem.at[2], at(x, p, seq)).start()

        return carry

    lax.fori_loop(0, 8, to_head, 0)

    @pl.when(grp == core)
    def _():
        zr[z] = zs[z % 8]
        perm_three = one_hot(256, 256, lambda o: (o % 16) * 16 + (o // 16 % 4) * 4 + o // 64)
        loads[2].wait()
        wait_bytes(zr.at[0:NZ - 1], rsem.at[2])
        lat = dot(perm_three, zr[...].reshape(256, 128)).astype(BF)
        value = sum(dot(lat[64 * i:64 * i + 64], vup[128 * i:128 * i + 128, :]) for i in range(4))
        vbuf[y] = value.astype(BF)

        def share(i, carry):
            p = (seq + i) % NS
            remote(vbuf.at[y], vbuf.at[y], vssem.at[i - 1], vrsem.at[y], at(x, z, p)).start()
            return carry

        lax.fori_loop(1, NS, share, 0)

    @pl.when(grp != core)
    def _():
        loads[2].wait()

    a, b = x // 2, x % 2
    u, v = z // 4, z % 4
    quad_r, quad_c = pl.ds(pl.multiple_of(a * 64, 64), 64), pl.ds(pl.multiple_of(b * 512, 512), 512)
    tile_r = pl.ds(pl.multiple_of(a * 64 + u * 16, 16), 16)
    tile_c = pl.ds(pl.multiple_of(b * 512 + v * 128, 128), 128)
    inner_r, inner_c = pl.ds(pl.multiple_of(u * 16, 16), 16), pl.ds(pl.multiple_of(v * 128, 128), 128)

    loads[3].wait()
    for c in range(2):
        for t in (2 * c, 2 * c + 1):
            @pl.when(jnp.logical_or(grp != core, y != t))
            def _():
                wait_bytes(vbuf.at[t], vrsem.at[t])
        os_[c] = dot(vbuf[2 * c:2 * c + 2].reshape(128, 128), wo[...]).astype(BF)
        x_peers(lambda p, device: remote(
            os_.at[c, pl.ds(pl.multiple_of(p // 2 * 64, 64), 64), pl.ds(pl.multiple_of(p % 2 * 512, 512), 512)],
            orx.at[c, x], ssem.at[4 + c], rsem.at[4 + c], device).start())
        orx[c, x] = os_[c, quad_r, quad_c]

    for c in range(2):
        wait_bytes(orx.at[c, 0:NX - 1], rsem.at[4 + c])
        oz[c] = sum(orx[c, i].astype(F32) for i in range(NX)).astype(BF)
        z_peers(lambda p, device: remote(
            oz.at[c, pl.ds(pl.multiple_of(p // 4 * 16, 16), 16), pl.ds(pl.multiple_of(p % 4 * 128, 128), 128)],
            orz.at[c, z], ssem.at[6 + c], rsem.at[6 + c], device).start())
        orz[c, z] = oz[c, inner_r, inner_c]

    loads[4].wait()
    gain = gain_ref[...]
    own_gain = gain_ref[:, tile_c]
    for c in range(2):
        own = one_hot(16, 256, lambda o: ((o // 8) * 32 + u * 8 + o % 8) * 4 + 2 * c + a)
        old = dot(own, res[:, tile_c])
        wait_bytes(orz.at[c, 0:NZ - 1], rsem.at[6 + c])
        stream = old + sum(orz[c, i].astype(F32) for i in range(NZ))
        st[c] = stream
        agb[c, tile_r, tile_c] = (stream * own_gain).astype(BF)
        z_peers(lambda p, device: remote(
            agb.at[c, tile_r, tile_c], agb.at[c, tile_r, tile_c],
            ssem.at[8 + c], rsem.at[8 + c], device).start())

    for c in range(2):
        wait_bytes(orz.at[c, 0:NZ - 1], rsem.at[8 + c])
        x_peers(lambda p, device: remote(
            agb.at[c, quad_r, quad_c], agb.at[c, quad_r, quad_c],
            ssem.at[10 + c], rsem.at[10 + c], device).start())

    inverse_gain = 1.0 / gain
    lane = iota((128, 128), 1)
    loads[5].wait()
    loads[6].wait()
    for c in range(2):
        wait_bytes(orx.at[c, 0:NX - 1], rsem.at[10 + c])
        scaled = agb[c]
        gs[c, :, 0:256] = dot(scaled, wg[...]).astype(BF)
        gs[c, :, 256:512] = dot(scaled, wu[...]).astype(BF)
        plain = scaled.astype(F32) * inverse_gain
        squares = jnp.sum(plain * plain, axis=1, keepdims=True)
        high = squares.astype(BF).astype(F32)
        gs[c, :, 512:640] = jnp.where(lane == 0, high, squares - high).astype(BF)

        def rows16(i):
            return pl.ds(pl.multiple_of(i * 16, 16), 16)

        s_peers(lambda p, device: remote(
            gs.at[c, rows16(p)], gr.at[c, seq], ssem.at[12 + c], rsem.at[12 + c], device).start())
        gr[c, seq] = gs[c, rows16(seq)]

    for c in range(2):
        wait_bytes(gr.at[c, 0:NS - 1], rsem.at[12 + c])
        sums = sum(gr[c, i].astype(F32) for i in range(NS))
        square = sums[:, 512:513] + sums[:, 513:514]
        inverse = lax.rsqrt(square * (1.0 / D) + 1e-06)
        gate = sums[:, 0:256] * inverse
        up = sums[:, 256:512] * inverse
        mine = rows16(seq)
        hb[c, mine] = (gate / (1.0 + jnp.exp(-gate)) * up).astype(BF)
        s_peers(lambda p, device: remote(
            hb.at[c, mine], hb.at[c, mine], ssem.at[14 + c], rsem.at[14 + c], device).start())

    loads[7].wait()
    perm_four = one_hot(256, 256, lambda o: (o // 2 % 8) * 32 + (o % 2) * 16 + o // 16)
    for c in range(2):
        wait_bytes(hb.at[c, 0:112], rsem.at[14 + c])
        part = dot(hb[c], wd[...])
        ds_[c] = part.astype(BF).reshape(2, 64, 1024)
        mine_r, mine_c = pl.ds(pl.multiple_of(u * 16, 16), 16), tile_c
        own = dot(hb[c, tile_r, :], wd[:, tile_c]) + st[c]
        ds_[c, a, mine_r, mine_c] = own.astype(BF)
        x_peers(lambda p, device: remote(
            ds_.at[c, :, pl.ds(pl.multiple_of(p * 16, 16), 16)], drx.at[c, x],
            ssem.at[16 + c], rsem.at[16 + c], device).start())
        drx[c, x] = ds_[c, :, pl.ds(pl.multiple_of(x * 16, 16), 16)]

    for c in range(2):
        wait_bytes(drx.at[c, 0:NX - 1], rsem.at[16 + c])
        summed = sum(drx[c, i].astype(F32) for i in range(NX)).astype(BF).reshape(32, 1024)
        stacked = jnp.concatenate([summed[:, 128 * i:128 * i + 128] for i in range(8)], axis=0)
        dz[c] = dot(perm_four, stacked).astype(BF).reshape(NZ, 16, 128)
        z_peers(lambda p, device: remote(
            dz.at[c, p], drz.at[c, z], ssem.at[18 + c], rsem.at[18 + c], device).start())
        drz[c, z] = dz[c, z]

    for c in range(2):
        wait_bytes(drz.at[c, 0:NZ - 1], rsem.at[18 + c])
        out_ref[c] = sum(drz[c, i].astype(F32) for i in range(NZ)).astype(BF)

    wait_bytes(arecv.at[0:NS - 1], ssem.at[0])
    wait_bytes(xr.at[0:NX - 1], ssem.at[1])

    @pl.when(grp == core)
    def _():
        wait_bytes(zs.at[0:7], ssem.at[2])

        def shared(i, carry):
            wait_bytes(vbuf.at[y], vssem.at[i - 1])
            return carry

        lax.fori_loop(1, NS, shared, 0)

    @pl.when(grp != core)
    def _():
        wait_bytes(zs, ssem.at[2])

    for c in range(2):
        wait_bytes(orx.at[c, 0:NX - 1], ssem.at[4 + c])
        wait_bytes(orz.at[c, 0:NZ - 1], ssem.at[6 + c])
        wait_bytes(orz.at[c, 0:NZ - 1], ssem.at[8 + c])
        wait_bytes(orx.at[c, 0:NX - 1], ssem.at[10 + c])
        wait_bytes(gr.at[c, 0:NS - 1], ssem.at[12 + c])
        wait_bytes(hb.at[c, 0:112], ssem.at[14 + c])
        wait_bytes(drx.at[c, 0:NX - 1], ssem.at[16 + c])
        wait_bytes(drz.at[c, 0:NZ - 1], ssem.at[18 + c])


def body(
    queries, new_latents, latent_cache, lengths, positions, value_up,
    output_weight, residual, norm_gain, gate_weight, up_weight, down_weight,
):
    cosines, sines = rope_tables(positions, 4, ROPE // 2)
    key_rope = rotate(new_latents[..., LATENT:].astype(F32), cosines, sines)
    new_keys = jnp.concatenate([new_latents[..., :LATENT], key_rope.astype(BF)], axis=-1)
    new_keys = jnp.pad(new_keys[0], ((0, 12), (0, 0)))
    both = jnp.concatenate([cosines[0], sines[0]], axis=0)
    table = jnp.concatenate([both, both], axis=1)
    vmem, hbm = pl.BlockSpec(memory_space=pltpu.VMEM), pl.BlockSpec(memory_space=pl.ANY)

    def buf(*shape, dtype=BF):
        return pltpu.VMEM(shape, dtype)

    out = pl.pallas_call(
        kernel,
        out_shape=jax.ShapeDtypeStruct((2, 16, 128), BF),
        in_specs=[pl.BlockSpec(memory_space=pltpu.SMEM), vmem, vmem, vmem] + [hbm] * 8,
        out_specs=vmem,
        scratch_shapes=[
            buf(256, 576), buf(256, 576), buf(512, 128), buf(128, 1024), buf(256, 1024),
            buf(1024, 256), buf(1024, 256), buf(256, 1024),
            buf(256, 640), buf(NS, 32, 640),
            buf(NX, 32, 128), buf(NX, 32, 128), buf(8, 16, 128), buf(NZ, 16, 128), buf(4, 64, 128),
            buf(2, 128, 1024), buf(2, NX, 64, 512), buf(2, 64, 512), buf(2, NZ, 16, 128),
            buf(2, 16, 128, dtype=F32), buf(2, 128, 1024),
            buf(2, 128, 640), buf(2, NS, 16, 640), buf(2, 128, 256),
            buf(2, 2, 64, 1024), buf(2, NX, 2, 16, 1024), buf(2, NZ, 16, 128), buf(2, NZ, 16, 128),
            pltpu.SemaphoreType.DMA((8,)),
            pltpu.SemaphoreType.DMA((20,)),
            pltpu.SemaphoreType.DMA((20,)),
            pltpu.SemaphoreType.DMA((NS - 1,)),
            pltpu.SemaphoreType.DMA((4,)),
        ],
        compiler_params=pltpu.CompilerParams(
            collective_id=0, has_side_effects=True, vmem_limit_bytes=40 * 1024 * 1024,
        ),
        cost_estimate=pl.CostEstimate(flops=10**9, bytes_accessed=4 * 10**6, transcendentals=10**5),
    )(
        lengths, table, new_keys, norm_gain.reshape(1, -1),
        queries.reshape(256, 576), latent_cache.reshape(256, 576), value_up.reshape(512, 128),
        output_weight, residual, gate_weight, up_weight, down_weight,
    )
    return out.reshape(2, 8, 2, 128).transpose(0, 2, 1, 3).reshape(4, 1024)


def solution(mesh):
    rows = ("grp", "hid")
    in_specs = (
        P(rows, None, None, None),
        P(rows, None, None),
        P(rows, "seq", None),
        P(rows),
        P(rows),
        P(rows, None, None),
        P(rows, "seq"),
        P(None, "seq"),
        P("seq"),
        P("seq", rows),
        P("seq", rows),
        P(rows, "seq"),
    )
    return jax.shard_map(body, mesh=mesh, in_specs=in_specs, out_specs=P(rows, "seq"), check_vma=False)
```

```python
import functools

import jax
import jax.numpy as jnp
import numpy as np
from jax import lax
from jax.experimental import pallas as pl
from jax.experimental.pallas import tpu as pltpu
from jax.sharding import PartitionSpec as P

D = 8192
LATENT = 512
ROPE = 64
NX, NZ, NS = 4, 16, 8
MESH = pl.DeviceIdType.MESH
BF = jnp.bfloat16
F32 = jnp.float32
score_scale = 192.0 ** (-0.5)


def dot(a, b):
    return lax.dot_general(a, b, (((1,), (0,)), ((), ())), preferred_element_type=F32)


def dot_t(a, b):
    return lax.dot_general(a, b, (((1,), (1,)), ((), ())), preferred_element_type=F32)


def iota(shape, axis):
    return lax.broadcasted_iota(jnp.int32, shape, axis)


def one_hot(rows, cols, source_of):
    return jnp.where(iota((rows, cols), 1) == source_of(iota((rows, cols), 0)), 1.0, 0.0).astype(BF)


def remote(src, dst, send_sem, recv_sem, device):
    return pltpu.make_async_remote_copy(
        src_ref=src, dst_ref=dst, send_sem=send_sem, recv_sem=recv_sem,
        device_id=device, device_id_type=MESH,
    )


def wait_bytes(ref, sem):
    pltpu.make_async_copy(ref, ref, sem).wait()


def kernel(
    freq_hbm, pos_hbm, len_hbm, new_hbm, gain_hbm,
    q_hbm, k_hbm, vup_hbm, wo_hbm, res_hbm, wg_hbm, wu_hbm, wd_hbm,
    out_ref,
    freq_ref, pos_ref, len_ref, new_ref, gain_ref,
    q, kt, vup, wo, res, wg, wu, wd,
    asend, arecv, zs, zr, vbuf, ob, orz, st, agb, gs, gr, hb,
    ds_, drx, dz, drz,
    lsem, ssem, rsem, fsem,
):
    grp, seq, hid = lax.axis_index("grp"), lax.axis_index("seq"), lax.axis_index("hid")
    x, z = hid // 8, grp * 8 + hid % 8
    y, core = seq // 2, seq % 2

    def at(xx, zz, ss):
        return (zz // 8, ss, xx * 8 + zz % 8)

    def each(count, me, fn):
        def step(i, carry):
            fn((me + i) % count)
            return carry
        lax.fori_loop(1, count, step, 0)

    def x_peers(fn):
        each(NX, x, lambda p: fn(p, at(p, z, seq)))

    def s_peers(fn):
        each(NS, seq, lambda p: fn(p, at(x, z, p)))

    def z_distance(i):
        return 8 + (1 - 2 * (i % 2)) * (i // 2)

    def z_peers(fn):
        def step(i, carry):
            p = (z + z_distance(i)) % NZ
            fn(p, at(x, p, seq))
            return carry
        lax.fori_loop(1, NZ, step, 0)

    def xs_peers(fn):
        for dx in (2, 1, 3, 0):
            def step(i, carry):
                p, r = (x + dx) % NX, (seq + i) % NS
                fn(p, at(p, z, r))
                return carry
            lax.fori_loop(1 if dx == 0 else 0, NS, step, 0)

    def rows(i, n):
        return pl.ds(pl.multiple_of(i * n, n), n)

    own_cols = rows(x, 256)
    loads = [
        pltpu.make_async_copy(a, b, lsem.at[i])
        for i, (a, b) in enumerate([
            (q_hbm, q), (k_hbm, kt), (vup_hbm, vup.at[x]), (wo_hbm.at[:, own_cols], wo.at[x]), (res_hbm, res),
            (wg_hbm, wg), (wu_hbm, wu), (wd_hbm, wd),
            (freq_hbm, freq_ref), (pos_hbm, pos_ref), (len_hbm, len_ref),
            (new_hbm, new_ref), (gain_hbm, gain_ref),
        ])
    ]
    for load in loads:
        load.start()

    barrier = pltpu.get_barrier_semaphore()

    def greet(p, device):
        pl.semaphore_signal(barrier, inc=1, device_id=device, device_id_type=MESH)

    xs_peers(greet)
    z_peers(greet)

    loads[8].wait()
    loads[9].wait()
    places = (pos_ref[0] + iota((8, 128), 0)).astype(F32)
    angles = places * freq_ref[...]
    cos_table, sin_table = jnp.cos(angles), jnp.sin(angles)
    loads[0].wait()
    rope_in = q[:, LATENT:]
    turn_r, turn_c = iota((ROPE, ROPE), 0), iota((ROPE, ROPE), 1)
    turn = jnp.where(
        turn_c == turn_r + 32, 1.0, jnp.where(turn_c == turn_r - 32, -1.0, 0.0)
    ).astype(BF)
    turned = dot(rope_in, turn)
    cosines = jnp.concatenate([jnp.broadcast_to(cos_table[t:t + 1, :ROPE], (64, ROPE)) for t in range(4)], axis=0)
    sines = jnp.concatenate([jnp.broadcast_to(sin_table[t:t + 1, :ROPE], (64, ROPE)) for t in range(4)], axis=0)
    q_rope = (rope_in.astype(F32) * cosines + turned * sines).astype(BF)
    q_lat = q[:, :LATENT]
    loads[11].wait()
    fresh = new_ref[...].astype(F32)
    fresh = jnp.concatenate([fresh, jnp.zeros((4, LATENT + ROPE), F32)], axis=0)
    fresh_in = fresh[:, LATENT:]
    fresh_turned = dot(fresh_in.astype(BF), turn)
    fresh_rope = fresh_in * cos_table[:, :ROPE] + fresh_turned * sin_table[:, :ROPE]
    new_lat = jnp.concatenate([fresh[:, :LATENT], jnp.zeros((8, LATENT), F32)], axis=0).astype(BF)
    new_rope = jnp.concatenate([fresh_rope, jnp.zeros((8, ROPE), F32)], axis=0).astype(BF)
    near = (dot_t(q_lat, new_lat) + dot_t(q_rope, new_rope)) * score_scale
    loads[1].wait()
    loads[10].wait()
    far = (dot(q_lat, kt[:LATENT, :]) + dot(q_rope, kt[LATENT:, :])) * score_scale
    usable = iota((256, 256), 1) + seq * 256 < len_ref[0]
    causal = iota((256, 16), 1) + seq * 1024 <= iota((256, 16), 0) // 64
    peak = jnp.maximum(
        jnp.max(jnp.where(usable, far, -1e30), axis=1, keepdims=True),
        jnp.max(jnp.where(causal, near, -1e30), axis=1, keepdims=True),
    )
    peak = jnp.floor(peak * (1.0 / 32.0)) * 32.0
    far_w = jnp.where(usable, jnp.exp(far - peak), 0.0)
    near_w = jnp.where(causal, jnp.exp(near - peak), 0.0)
    total = jnp.sum(far_w, axis=1, keepdims=True) + jnp.sum(near_w, axis=1, keepdims=True)
    mixture = dot_t(far_w.astype(BF), kt[:LATENT, :]) + dot(near_w.astype(BF), new_lat)
    asend[:, :LATENT] = mixture.astype(BF)
    lane = iota((256, 128), 1)
    high = total.astype(BF).astype(F32)
    asend[:, LATENT:] = jnp.where(
        lane == 0, peak, jnp.where(lane == 1, high, total - high)
    ).astype(BF)

    pl.semaphore_wait(barrier, (NX * NS - 1) + (NZ - 1))
    s_peers(lambda p, device: remote(
        asend.at[rows(p, 32)], arecv.at[seq], ssem.at[0], rsem.at[0], device).start())

    x_peers(lambda p, device: remote(
        vup_hbm, vup.at[x], ssem.at[1], rsem.at[1], device).start())
    x_peers(lambda p, device: remote(
        wo_hbm.at[:, rows(p, 256)], wo.at[x], ssem.at[2], rsem.at[2], device).start())

    arecv[seq] = asend[rows(seq, 32)]
    perm_one = one_hot(128, 128, lambda o: (o % 4) * 32 + (o // 4 % 4) * 8 + o // 16)
    perm_two = one_hot(256, 256, lambda o: (o % 16) * 16 + o // 16)
    wait_bytes(arecv.at[0:NS - 1], rsem.at[0])

    aux = [arecv[i, :, LATENT:].astype(F32) for i in range(NS)]
    top = functools.reduce(jnp.maximum, [a[:, 0:1] for a in aux])
    factors = [jnp.exp(a[:, 0:1] - top) for a in aux]
    totals = sum(f * (a[:, 1:2] + a[:, 2:3]) for f, a in zip(factors, aux))
    mixed = sum(f * arecv[i, :, :LATENT].astype(F32) for i, f in enumerate(factors))
    heads = (mixed / totals).astype(BF)

    stacked = jnp.concatenate([heads[:, 128 * i:128 * i + 128] for i in range(4)], axis=0)
    zs[...] = dot(perm_one, stacked).astype(BF).reshape(8, 16, 128)

    def to_head(j, carry):
        p = core * 8 + j

        @pl.when(p != z)
        def _():
            remote(zs.at[j], zr.at[z], ssem.at[3], rsem.at[3], at(x, p, seq)).start()

        return carry

    lax.fori_loop(0, 8, to_head, 0)
    loads[2].wait()
    wait_bytes(vup.at[0:NX - 1], rsem.at[1])
    value_rows = rows(y * 4 + x, 16)

    @pl.when(grp == core)
    def _():
        zr[z] = zs[z % 8]
        wait_bytes(zr.at[0:NZ - 1], rsem.at[3])
        lat = dot(perm_two, zr[...].reshape(256, 128)).astype(BF)
        for i in range(NX):
            wide = jnp.concatenate([lat[64 * i + 16 * n:64 * i + 16 * n + 16] for n in range(4)], axis=1)
            vbuf[value_rows, 128 * i:128 * i + 128] = dot(wide, vup[i]).astype(BF)
        xs_peers(lambda p, device: remote(
            vbuf.at[value_rows], vbuf.at[value_rows], ssem.at[4], rsem.at[4], device).start())

    loads[3].wait()
    wait_bytes(wo.at[0:NX - 1], rsem.at[2])

    @pl.when(grp == core)
    def _():
        wait_bytes(vbuf.at[0:240], rsem.at[4])

    @pl.when(grp != core)
    def _():
        wait_bytes(vbuf, rsem.at[4])

    ob[...] = dot(vbuf[...], wo[...].reshape(512, 256)).astype(BF)
    z_peers(lambda p, device: remote(
        ob.at[rows(p, 16)], orz.at[z], ssem.at[5], rsem.at[5], device).start())
    tile = rows(z, 16)
    orz[z] = ob[tile]
    loads[4].wait()
    loads[12].wait()
    gain = gain_ref[...]
    own = one_hot(16, 256, lambda o: ((o // 8) * 32 + (z % 4) * 8 + o % 8) * 4 + z // 4)
    old = dot(own, res[:, own_cols])
    wait_bytes(orz.at[0:NZ - 1], rsem.at[5])
    stream = old + sum(orz[i].astype(F32) for i in range(NZ))
    st[...] = stream
    agb[tile, own_cols] = (stream * gain_ref[:, own_cols]).astype(BF)
    z_peers(lambda p, device: remote(
        agb.at[tile, own_cols], agb.at[tile, own_cols], ssem.at[6], fsem.at[z], device).start())

    def forward(p):
        piece = agb.at[rows(p, 16), own_cols]
        x_peers(lambda _, device: remote(piece, piece, ssem.at[7], rsem.at[7], device).start())

    def arrived(i, carry):
        p = (z + z_distance(NZ - i)) % NZ
        wait_bytes(agb.at[rows(p, 16), own_cols], fsem.at[p])
        forward(p)
        return carry

    forward(z)
    lax.fori_loop(1, NZ, arrived, 0)

    inverse_gain = 1.0 / gain
    lane = iota((256, 128), 1)
    loads[5].wait()
    loads[6].wait()
    wait_bytes(agb.at[0:192], rsem.at[7])
    scaled = agb[...]
    gs[:, 0:256] = dot(scaled, wg[...]).astype(BF)
    gs[:, 256:512] = dot(scaled, wu[...]).astype(BF)
    plain = scaled.astype(F32) * inverse_gain
    squares = jnp.sum(plain * plain, axis=1, keepdims=True)
    high = squares.astype(BF).astype(F32)
    gs[:, 512:640] = jnp.where(lane == 0, high, squares - high).astype(BF)
    s_peers(lambda p, device: remote(
        gs.at[rows(p, 32)], gr.at[seq], ssem.at[8], rsem.at[8], device).start())
    mine = rows(seq, 32)
    gr[seq] = gs[mine]

    wait_bytes(gr.at[0:NS - 1], rsem.at[8])
    sums = sum(gr[i].astype(F32) for i in range(NS))
    square = sums[:, 512:513] + sums[:, 513:514]
    inverse = lax.rsqrt(square * (1.0 / D) + 1e-06)
    gate = sums[:, 0:256] * inverse
    up = sums[:, 256:512] * inverse
    hb[mine] = (gate / (1.0 + jnp.exp(-gate)) * up).astype(BF)
    s_peers(lambda p, device: remote(
        hb.at[mine], hb.at[mine], ssem.at[9], rsem.at[9], device).start())

    loads[7].wait()
    perm_four = one_hot(256, 256, lambda o: (o // 2 % 8) * 32 + (o % 2) * 16 + o // 16)
    wait_bytes(hb.at[0:224], rsem.at[9])
    for c in range(2):
        ds_[c] = dot(hb[128 * c:128 * c + 128], wd[...]).astype(BF).reshape(2, 64, 1024)

        @pl.when(grp == c)
        def _():
            own = dot(hb[tile], wd[:, own_cols]) + st[...]
            ds_[c, z // 4 % 2, rows(z % 4, 16), own_cols] = own.astype(BF)

        x_peers(lambda p, device: remote(
            ds_.at[c, :, pl.ds(pl.multiple_of(p * 16, 16), 16)], drx.at[c, x],
            ssem.at[10 + c], rsem.at[10 + c], device).start())
        drx[c, x] = ds_[c, :, pl.ds(pl.multiple_of(x * 16, 16), 16)]

    for c in range(2):
        wait_bytes(drx.at[c, 0:NX - 1], rsem.at[10 + c])
        summed = sum(drx[c, i].astype(F32) for i in range(NX)).astype(BF).reshape(32, 1024)
        stacked = jnp.concatenate([summed[:, 128 * i:128 * i + 128] for i in range(8)], axis=0)
        dz[c] = dot(perm_four, stacked).astype(BF).reshape(NZ, 16, 128)
        z_peers(lambda p, device: remote(
            dz.at[c, p], drz.at[c, z], ssem.at[12 + c], rsem.at[12 + c], device).start())
        drz[c, z] = dz[c, z]

    for c in range(2):
        wait_bytes(drz.at[c, 0:NZ - 1], rsem.at[12 + c])
        final = sum(drz[c, i].astype(F32) for i in range(NZ)).astype(BF)
        for i in range(8):
            out_ref[2 * c:2 * c + 2, 128 * i:128 * i + 128] = final[2 * i:2 * i + 2]

    wait_bytes(arecv.at[0:NS - 1], ssem.at[0])
    wait_bytes(vup.at[0:NX - 1], ssem.at[1])
    wait_bytes(wo.at[0:NX - 1], ssem.at[2])

    @pl.when(grp == core)
    def _():
        wait_bytes(zs.at[0:7], ssem.at[3])
        wait_bytes(wg.at[0:992], ssem.at[4])

    @pl.when(grp != core)
    def _():
        wait_bytes(zs, ssem.at[3])

    wait_bytes(orz.at[0:NZ - 1], ssem.at[5])
    wait_bytes(orz.at[0:NZ - 1], ssem.at[6])
    wait_bytes(agb.at[0:192], ssem.at[7])
    wait_bytes(gr.at[0:NS - 1], ssem.at[8])
    wait_bytes(hb.at[0:224], ssem.at[9])
    for c in range(2):
        wait_bytes(drx.at[c, 0:NX - 1], ssem.at[10 + c])
        wait_bytes(drz.at[c, 0:NZ - 1], ssem.at[12 + c])


def body(
    queries, new_latents, latent_cache, lengths, positions, value_up,
    output_weight, residual, norm_gain, gate_weight, up_weight, down_weight,
):
    halfwidth = ROPE // 2
    frequency = 1000000.0 ** (-np.arange(halfwidth, dtype=np.float64) / halfwidth)
    frequency = jnp.asarray(np.tile(frequency, 4)[None, :], F32)
    vmem, hbm = pl.BlockSpec(memory_space=pltpu.VMEM), pl.BlockSpec(memory_space=pltpu.HBM)

    def buf(*shape, dtype=BF):
        return pltpu.VMEM(shape, dtype)

    return pl.pallas_call(
        kernel,
        out_shape=jax.ShapeDtypeStruct((4, 1024), BF),
        in_specs=[hbm] * 13,
        out_specs=vmem,
        scratch_shapes=[
            buf(1, 128, dtype=F32), pltpu.SMEM((1,), jnp.int32), pltpu.SMEM((1,), jnp.int32),
            buf(4, 576), buf(1, 1024, dtype=F32),
            buf(256, 576), buf(576, 256), buf(NX, 512, 128), buf(NX, 128, 256), buf(256, 1024),
            buf(1024, 256), buf(1024, 256), buf(256, 1024),
            buf(256, 640), buf(NS, 32, 640), buf(8, 16, 128), buf(NZ, 16, 128),
            buf(256, 512), buf(256, 256), buf(NZ, 16, 256), buf(16, 256, dtype=F32), buf(256, 1024),
            buf(256, 640), buf(NS, 32, 640), buf(256, 256),
            buf(2, 2, 64, 1024), buf(2, NX, 2, 16, 1024), buf(2, NZ, 16, 128), buf(2, NZ, 16, 128),
            pltpu.SemaphoreType.DMA((13,)),
            pltpu.SemaphoreType.DMA((14,)),
            pltpu.SemaphoreType.DMA((14,)),
            pltpu.SemaphoreType.DMA((NZ,)),
        ],
        compiler_params=pltpu.CompilerParams(
            collective_id=0, has_side_effects=True, vmem_limit_bytes=56 * 1024 * 1024,
        ),
        cost_estimate=pl.CostEstimate(flops=10**9, bytes_accessed=4 * 10**6, transcendentals=10**5),
    )(
        frequency, positions, lengths, new_latents.reshape(4, 576), norm_gain.reshape(1, -1),
        queries.reshape(256, 576), jnp.swapaxes(latent_cache.reshape(256, 576), 0, 1), value_up.reshape(512, 128),
        output_weight, residual, gate_weight, up_weight, down_weight,
    )


def solution(mesh):
    rows = ("grp", "hid")
    in_specs = (
        P(rows, None, None, None),
        P(rows, None, None),
        P(rows, "seq", None),
        P(rows),
        P(rows),
        P(rows, None, None),
        P(rows, "seq"),
        P(None, "seq"),
        P("seq"),
        P("seq", rows),
        P("seq", rows),
        P(rows, "seq"),
    )
    return jax.shard_map(body, mesh=mesh, in_specs=in_specs, out_specs=P(rows, "seq"), check_vma=False)
```

```python
import functools

import jax
import jax.numpy as jnp
import numpy as np
from jax import lax
from jax.experimental import pallas as pl
from jax.experimental.pallas import tpu as pltpu
from jax.sharding import PartitionSpec as P

D = 8192
LATENT = 512
ROPE = 64
NX, NZ, NS = 4, 16, 8
MESH = pl.DeviceIdType.MESH
BF = jnp.bfloat16
F32 = jnp.float32
score_scale = 192.0 ** (-0.5)


def dot(a, b):
    return lax.dot_general(a, b, (((1,), (0,)), ((), ())), preferred_element_type=F32)


def dot_t(a, b):
    return lax.dot_general(a, b, (((1,), (1,)), ((), ())), preferred_element_type=F32)


def iota(shape, axis):
    return lax.broadcasted_iota(jnp.int32, shape, axis)


def one_hot(rows, cols, source_of):
    return jnp.where(iota((rows, cols), 1) == source_of(iota((rows, cols), 0)), 1.0, 0.0).astype(BF)


def remote(src, dst, send_sem, recv_sem, device):
    return pltpu.make_async_remote_copy(
        src_ref=src, dst_ref=dst, send_sem=send_sem, recv_sem=recv_sem,
        device_id=device, device_id_type=MESH,
    )


def wait_bytes(ref, sem):
    pltpu.make_async_copy(ref, ref, sem).wait()


def kernel(
    freq_hbm, pos_hbm, len_hbm, new_hbm, gain_hbm,
    q_hbm, k_hbm, vup_hbm, wo_hbm, res_hbm, wg_hbm, wu_hbm, wd_hbm,
    out_ref,
    freq_ref, pos_ref, len_ref, new_ref, gain_ref,
    q, kt, vup, wo, res, wg, wu, wd,
    asend, arecv, zs, zr, vbuf, ob, orz, st, agb, gs, gr, hb,
    ds_, drx, dz, drz,
    lsem, ssem, rsem, vsem, fsem,
):
    grp, seq, hid = lax.axis_index("grp"), lax.axis_index("seq"), lax.axis_index("hid")
    x, z = hid // 8, grp * 8 + hid % 8
    y, core = seq // 2, seq % 2

    def at(xx, zz, ss):
        return (zz // 8, ss, xx * 8 + zz % 8)

    def each(count, me, fn):
        def step(i, carry):
            fn((me + i) % count)
            return carry
        lax.fori_loop(1, count, step, 0)

    def x_peers(fn):
        each(NX, x, lambda p: fn(p, at(p, z, seq)))

    def s_peers(fn):
        each(NS, seq, lambda p: fn(p, at(x, z, p)))

    def z_distance(i):
        return 8 + (1 - 2 * (i % 2)) * (i // 2)

    def z_peers(fn):
        def step(i, carry):
            p = (z + z_distance(i)) % NZ
            fn(p, at(x, p, seq))
            return carry
        lax.fori_loop(1, NZ, step, 0)

    def xs_peers(fn):
        for dx in (2, 1, 3, 0):
            def step(i, carry):
                p, r = (x + dx) % NX, (seq + i) % NS
                fn(p, at(p, z, r))
                return carry
            lax.fori_loop(1 if dx == 0 else 0, NS, step, 0)

    def rows(i, n):
        return pl.ds(pl.multiple_of(i * n, n), n)

    own_cols = rows(x, 256)
    barrier = pltpu.get_barrier_semaphore()

    def greet(p, device):
        pl.semaphore_signal(barrier, inc=1, device_id=device, device_id_type=MESH)

    z_peers(greet)
    xs_peers(greet)

    loads = [
        pltpu.make_async_copy(a, b, lsem.at[i])
        for i, (a, b) in enumerate([
            (q_hbm, q), (k_hbm, kt), (vup_hbm, vup.at[x]), (wo_hbm.at[:, own_cols], wo.at[x]), (res_hbm, res),
            (wg_hbm, wg), (wu_hbm, wu), (wd_hbm, wd),
            (freq_hbm, freq_ref), (pos_hbm, pos_ref), (len_hbm, len_ref),
            (new_hbm, new_ref), (gain_hbm, gain_ref),
        ])
    ]
    early = (1, 0, 9, 8, 11, 10)
    for i in early:
        loads[i].start()

    loads[8].wait()
    loads[9].wait()
    places = (jnp.broadcast_to(pos_ref[...], (8, 128)) + iota((8, 128), 0)).astype(F32)
    angles = places * freq_ref[...]
    cos_table, sin_table = jnp.cos(angles), jnp.sin(angles)
    loads[0].wait()
    rope_in = q[:, LATENT:]
    turn_r, turn_c = iota((ROPE, ROPE), 0), iota((ROPE, ROPE), 1)
    turn = jnp.where(
        turn_c == turn_r + 32, 1.0, jnp.where(turn_c == turn_r - 32, -1.0, 0.0)
    ).astype(BF)
    turned = dot(rope_in, turn)
    cosines = jnp.concatenate([jnp.broadcast_to(cos_table[t:t + 1, :ROPE], (64, ROPE)) for t in range(4)], axis=0)
    sines = jnp.concatenate([jnp.broadcast_to(sin_table[t:t + 1, :ROPE], (64, ROPE)) for t in range(4)], axis=0)
    q_rope = (rope_in.astype(F32) * cosines + turned * sines).astype(BF)
    q_lat = q[:, :LATENT]
    loads[11].wait()
    fresh = new_ref[...].astype(F32)
    fresh = jnp.concatenate([fresh, jnp.zeros((4, LATENT + ROPE), F32)], axis=0)
    fresh_in = fresh[:, LATENT:]
    fresh_turned = dot(fresh_in.astype(BF), turn)
    fresh_rope = fresh_in * cos_table[:, :ROPE] + fresh_turned * sin_table[:, :ROPE]
    new_lat = jnp.concatenate([fresh[:, :LATENT], jnp.zeros((8, LATENT), F32)], axis=0).astype(BF)
    new_rope = jnp.concatenate([fresh_rope, jnp.zeros((8, ROPE), F32)], axis=0).astype(BF)
    near = (dot_t(q_lat, new_lat) + dot_t(q_rope, new_rope)) * score_scale
    loads[1].wait()
    for i in range(13):
        if i not in early:
            loads[i].start()
    loads[10].wait()
    far = (dot(q_lat, kt[:LATENT, :]) + dot(q_rope, kt[LATENT:, :])) * score_scale
    usable = iota((256, 256), 1) + seq * 256 < jnp.broadcast_to(len_ref[...], (256, 256))
    causal = iota((256, 16), 1) + seq * 1024 <= iota((256, 16), 0) // 64
    peak = jnp.maximum(
        jnp.max(jnp.where(usable, far, -1e30), axis=1, keepdims=True),
        jnp.max(jnp.where(causal, near, -1e30), axis=1, keepdims=True),
    )
    peak = jnp.floor(peak * (1.0 / 32.0)) * 32.0
    far_w = jnp.where(usable, jnp.exp(far - peak), 0.0)
    near_w = jnp.where(causal, jnp.exp(near - peak), 0.0)
    total = jnp.sum(far_w, axis=1, keepdims=True) + jnp.sum(near_w, axis=1, keepdims=True)
    mixture = dot_t(far_w.astype(BF), kt[:LATENT, :]) + dot(near_w.astype(BF), new_lat)
    asend[:, :LATENT] = mixture.astype(BF)
    lane = iota((256, 128), 1)
    high = total.astype(BF).astype(F32)
    asend[:, LATENT:] = jnp.where(
        lane == 0, peak, jnp.where(lane == 1, high, total - high)
    ).astype(BF)

    pl.semaphore_wait(barrier, (NX * NS - 1) + (NZ - 1))
    s_peers(lambda p, device: remote(
        asend.at[rows(p, 32)], arecv.at[seq], ssem.at[0], rsem.at[0], device).start())

    x_peers(lambda p, device: remote(
        vup_hbm, vup.at[x], ssem.at[1], rsem.at[1], device).start())
    x_peers(lambda p, device: remote(
        wo_hbm.at[:, rows(p, 256)], wo.at[x], ssem.at[2], rsem.at[2], device).start())

    arecv[seq] = asend[rows(seq, 32)]
    perm_one = one_hot(128, 128, lambda o: (o % 4) * 32 + (o // 4 % 4) * 8 + o // 16)
    perm_two = one_hot(256, 256, lambda o: (o % 16) * 16 + o // 16)
    wait_bytes(arecv.at[0:NS - 1], rsem.at[0])

    aux = [arecv[i, :, LATENT:].astype(F32) for i in range(NS)]
    top = functools.reduce(jnp.maximum, [a[:, 0:1] for a in aux])
    factors = [jnp.exp(a[:, 0:1] - top) for a in aux]
    totals = sum(f * (a[:, 1:2] + a[:, 2:3]) for f, a in zip(factors, aux))
    mixed = sum(f * arecv[i, :, :LATENT].astype(F32) for i, f in enumerate(factors))
    heads = (mixed / totals).astype(BF)

    stacked = jnp.concatenate([heads[:, 128 * i:128 * i + 128] for i in range(4)], axis=0)
    zs[...] = dot(perm_one, stacked).astype(BF).reshape(8, 16, 128)

    def to_head(j, carry):
        p = core * 8 + j

        @pl.when(p != z)
        def _():
            remote(zs.at[j], zr.at[z], ssem.at[3], rsem.at[3], at(x, p, seq)).start()

        return carry

    lax.fori_loop(0, 8, to_head, 0)
    loads[2].wait()
    wait_bytes(vup.at[0:NX - 1], rsem.at[1])
    value_rows = rows(y * 4 + x, 16)

    @pl.when(grp == core)
    def _():
        zr[z] = zs[z % 8]
        wait_bytes(zr.at[0:NZ - 1], rsem.at[3])
        lat = dot(perm_two, zr[...].reshape(256, 128)).astype(BF)
        for i in range(NX):
            wide = jnp.concatenate([lat[64 * i + 16 * n:64 * i + 16 * n + 16] for n in range(4)], axis=1)
            vbuf[value_rows, 128 * i:128 * i + 128] = dot(wide, vup[i]).astype(BF)
        other = at(x, z, y * 2 + 1 - core)
        steps = sorted(
            ((dx, dy) for dx in range(NX) for dy in range(4) if dx or dy),
            key=lambda d: min(d[0], 4 - d[0]) + min(d[1], 4 - d[1]),
        )
        for dx, dy in steps[::-1]:
            remote(
                vbuf.at[value_rows], vbuf.at[value_rows], ssem.at[4], vsem.at[y],
                at((x + dx) % 4, z, (y + dy) % 4 * 2 + core),
            ).start()

        for dt in (0, 1, 3, 2):
            t = (y + dt) % 4
            piece = vbuf.at[rows(t, 64)]
            if dt == 0:
                wait_bytes(vbuf.at[0:48], vsem.at[t])
            else:
                wait_bytes(piece, vsem.at[t])
            remote(piece, piece, ssem.at[4], rsem.at[4], other).start()

    loads[3].wait()
    wait_bytes(wo.at[0:NX - 1], rsem.at[2])

    @pl.when(grp != core)
    def _():
        wait_bytes(vbuf, rsem.at[4])

    ob[...] = dot(vbuf[...], wo[...].reshape(512, 256)).astype(BF)
    z_peers(lambda p, device: remote(
        ob.at[rows(p, 16)], orz.at[z], ssem.at[5], rsem.at[5], device).start())
    tile = rows(z, 16)
    orz[z] = ob[tile]
    loads[4].wait()
    loads[12].wait()
    gain = gain_ref[...]
    own = one_hot(16, 256, lambda o: ((o // 8) * 32 + (z % 4) * 8 + o % 8) * 4 + z // 4)
    old = dot(own, res[:, own_cols])
    wait_bytes(orz.at[0:NZ - 1], rsem.at[5])
    stream = old + sum(orz[i].astype(F32) for i in range(NZ))
    st[...] = stream
    agb[tile, own_cols] = (stream * gain_ref[:, own_cols]).astype(BF)
    z_peers(lambda p, device: remote(
        agb.at[tile, own_cols], agb.at[tile, own_cols], ssem.at[6], fsem.at[z // 4], device).start())

    t_own, side = z // 4, z % 4 // 2
    order = [t_own, (t_own + 3 + 2 * side) % 4, (t_own + 1 + 2 * side) % 4, (t_own + 2) % 4]

    for n, t in enumerate(order):
        piece = agb.at[rows(t, 64), own_cols]
        if n == 0:
            wait_bytes(orz.at[0:3], fsem.at[t])
        else:
            wait_bytes(piece, fsem.at[t])
        x_peers(lambda _, device: remote(
            piece, piece, ssem.at[7], rsem.at[16 + n // 2], device).start())

    inverse_gain = 1.0 / gain
    lane = iota((128, 128), 1)
    loads[5].wait()
    loads[6].wait()
    for c in range(2):
        wait_bytes(agb.at[0:96], rsem.at[16 + c])
        scaled = jnp.concatenate([agb[rows(t, 64)] for t in order[2 * c:2 * c + 2]], axis=0)
        gs[c, :, 0:256] = dot(scaled, wg[...]).astype(BF)
        gs[c, :, 256:512] = dot(scaled, wu[...]).astype(BF)
        plain = scaled.astype(F32) * inverse_gain
        squares = jnp.sum(plain * plain, axis=1, keepdims=True)
        high = squares.astype(BF).astype(F32)
        gs[c, :, 512:640] = jnp.where(lane == 0, high, squares - high).astype(BF)
        s_peers(lambda p, device: remote(
            gs.at[c, rows(p, 16)], gr.at[c, seq], ssem.at[8 + c], rsem.at[8 + c], device).start())
        gr[c, seq] = gs[c, rows(seq, 16)]

    mine = rows(seq, 16)
    for c in range(2):
        wait_bytes(gr.at[c, 0:NS - 1], rsem.at[8 + c])
        sums = sum(gr[c, i].astype(F32) for i in range(NS))
        square = sums[:, 512:513] + sums[:, 513:514]
        inverse = lax.rsqrt(square * (1.0 / D) + 1e-06)
        gate = sums[:, 0:256] * inverse
        up = sums[:, 256:512] * inverse
        hb[c, mine] = (gate / (1.0 + jnp.exp(-gate)) * up).astype(BF)
        s_peers(lambda p, device: remote(
            hb.at[c, mine], hb.at[c, mine], ssem.at[10 + c], rsem.at[10 + c], device).start())

    loads[7].wait()
    perm_three = one_hot(256, 256, lambda o: (o % 8) * 32 + (o // 8 % 2) * 16 + o // 16)
    for c in range(2):
        wait_bytes(hb.at[c, 0:112], rsem.at[10 + c])
        ds_[c] = dot(hb[c], wd[...]).astype(BF).reshape(2, 64, 1024)
        if c == 0:
            place = rows(z % 4, 16)
            own = dot(hb[0, place], wd[:, own_cols]) + st[...]
            ds_[0, 0, place, own_cols] = own.astype(BF)
        x_peers(lambda p, device: remote(
            ds_.at[c, :, pl.ds(pl.multiple_of(p * 16, 16), 16)], drx.at[c, x],
            ssem.at[12 + c], rsem.at[12 + c], device).start())
        drx[c, x] = ds_[c, :, pl.ds(pl.multiple_of(x * 16, 16), 16)]

    for c in range(2):
        wait_bytes(drx.at[c, 0:NX - 1], rsem.at[12 + c])
        summed = sum(drx[c, i].astype(F32) for i in range(NX)).astype(BF).reshape(32, 1024)
        stacked = jnp.concatenate([summed[:, 128 * i:128 * i + 128] for i in range(8)], axis=0)
        dz[c] = dot(perm_three, stacked).astype(BF).reshape(NZ, 16, 128)
        z_peers(lambda p, device: remote(
            dz.at[c, p], drz.at[c, z], ssem.at[14 + c], rsem.at[14 + c], device).start())
        drz[c, z] = dz[c, z]

    for c in range(2):
        wait_bytes(drz.at[c, 0:NZ - 1], rsem.at[14 + c])
    final = [0.0] * 4
    for i in range(NZ):
        turn = [i // 4, (i // 4 + 3 + 2 * (i % 4 // 2)) % 4, (i // 4 + 1 + 2 * (i % 4 // 2)) % 4, (i // 4 + 2) % 4]
        for c in range(2):
            part = drz[c, i].astype(F32)
            for n in range(2):
                final[turn[2 * c + n]] += part[8 * n:8 * n + 8]
    for i in range(8):
        out_ref[:, 128 * i:128 * i + 128] = jnp.concatenate([f[i:i + 1] for f in final], axis=0).astype(BF)

    wait_bytes(arecv.at[0:NS - 1], ssem.at[0])
    wait_bytes(vup.at[0:NX - 1], ssem.at[1])
    wait_bytes(wo.at[0:NX - 1], ssem.at[2])

    @pl.when(grp == core)
    def _():
        wait_bytes(zs.at[0:7], ssem.at[3])
        wait_bytes(wg.at[0:992], ssem.at[4])

    @pl.when(grp != core)
    def _():
        wait_bytes(zs, ssem.at[3])

    wait_bytes(orz.at[0:NZ - 1], ssem.at[5])
    wait_bytes(orz.at[0:NZ - 1], ssem.at[6])
    wait_bytes(agb.at[0:192], ssem.at[7])
    for c in range(2):
        wait_bytes(gr.at[c, 0:NS - 1], ssem.at[8 + c])
        wait_bytes(hb.at[c, 0:112], ssem.at[10 + c])
        wait_bytes(drx.at[c, 0:NX - 1], ssem.at[12 + c])
        wait_bytes(drz.at[c, 0:NZ - 1], ssem.at[14 + c])


def body(
    queries, new_latents, latent_cache, lengths, positions, value_up,
    output_weight, residual, norm_gain, gate_weight, up_weight, down_weight,
):
    halfwidth = ROPE // 2
    frequency = 1000000.0 ** (-np.arange(halfwidth, dtype=np.float64) / halfwidth)
    frequency = jnp.asarray(np.tile(frequency, 4)[None, :], F32)
    vmem, hbm = pl.BlockSpec(memory_space=pltpu.VMEM), pl.BlockSpec(memory_space=pltpu.HBM)

    def buf(*shape, dtype=BF):
        return pltpu.VMEM(shape, dtype)

    return pl.pallas_call(
        kernel,
        out_shape=pltpu.VMEM((4, 1024), BF),
        in_specs=[hbm] * 13,
        out_specs=vmem,
        scratch_shapes=[
            buf(1, 128, dtype=F32), buf(1, 1, dtype=jnp.int32), buf(1, 1, dtype=jnp.int32),
            buf(4, 576), buf(1, 1024, dtype=F32),
            buf(256, 576), buf(576, 256), buf(NX, 512, 128), buf(NX, 128, 256), buf(256, 1024),
            buf(1024, 256), buf(1024, 256), buf(256, 1024),
            buf(256, 640), buf(NS, 32, 640), buf(8, 16, 128), buf(NZ, 16, 128),
            buf(256, 512), buf(256, 256), buf(NZ, 16, 256), buf(16, 256, dtype=F32), buf(256, 1024),
            buf(2, 128, 640), buf(2, NS, 16, 640), buf(2, 128, 256),
            buf(2, 2, 64, 1024), buf(2, NX, 2, 16, 1024), buf(2, NZ, 16, 128), buf(2, NZ, 16, 128),
            pltpu.SemaphoreType.DMA((13,)),
            pltpu.SemaphoreType.DMA((16,)),
            pltpu.SemaphoreType.DMA((18,)),
            pltpu.SemaphoreType.DMA((4,)),
            pltpu.SemaphoreType.DMA((4,)),
        ],
        compiler_params=pltpu.CompilerParams(
            collective_id=0, has_side_effects=True, vmem_limit_bytes=56 * 1024 * 1024,
        ),
        cost_estimate=pl.CostEstimate(flops=10**9, bytes_accessed=4 * 10**6, transcendentals=10**5),
    )(
        frequency, positions.reshape(1, 1), lengths.reshape(1, 1), new_latents.reshape(4, 576), norm_gain.reshape(1, -1),
        queries.reshape(256, 576), jnp.swapaxes(latent_cache.reshape(256, 576), 0, 1), value_up.reshape(512, 128),
        output_weight, residual, gate_weight, up_weight, down_weight,
    )


def solution(mesh):
    rows = ("grp", "hid")
    in_specs = (
        P(rows, None, None, None),
        P(rows, None, None),
        P(rows, "seq", None),
        P(rows),
        P(rows),
        P(rows, None, None),
        P(rows, "seq"),
        P(None, "seq"),
        P("seq"),
        P("seq", rows),
        P("seq", rows),
        P(rows, "seq"),
    )
    return jax.shard_map(body, mesh=mesh, in_specs=in_specs, out_specs=P(rows, "seq"), check_vma=False)
```

```python
import functools

import jax
import jax.numpy as jnp
import numpy as np
from jax import lax
from jax.experimental import pallas as pl
from jax.experimental.pallas import tpu as pltpu
from jax.sharding import PartitionSpec as P

D = 8192
LATENT = 512
ROPE = 64
NX, NZ, NS = 4, 16, 8
MESH = pl.DeviceIdType.MESH
BF = jnp.bfloat16
F32 = jnp.float32
score_scale = 192.0 ** (-0.5)


def dot(a, b):
    return lax.dot_general(a, b, (((1,), (0,)), ((), ())), preferred_element_type=F32)


def dot_t(a, b):
    return lax.dot_general(a, b, (((1,), (1,)), ((), ())), preferred_element_type=F32)


def iota(shape, axis):
    return lax.broadcasted_iota(jnp.int32, shape, axis)


def one_hot(rows, cols, source_of):
    return jnp.where(iota((rows, cols), 1) == source_of(iota((rows, cols), 0)), 1.0, 0.0).astype(BF)


def remote(src, dst, send_sem, recv_sem, device):
    return pltpu.make_async_remote_copy(
        src_ref=src, dst_ref=dst, send_sem=send_sem, recv_sem=recv_sem,
        device_id=device, device_id_type=MESH,
    )


def wait_bytes(ref, sem):
    pltpu.make_async_copy(ref, ref, sem).wait()


def kernel(
    freq_hbm, pos_hbm, len_hbm, new_hbm, gain_hbm,
    q_hbm, k_hbm, vup_hbm, wo_hbm, res_hbm, wg_hbm, wu_hbm, wd_hbm,
    out_ref,
    freq_ref, pos_ref, len_ref, new_ref, gain_ref,
    q, kt, vup, wo, res, wg, wu, wd,
    asend, arecv, zs, zr, vbuf, ob, orz, st, agb, gs, gr, hb, ds_, drx, dz, drz,
    lsem, ssem, rsem, fsem,
):
    grp, seq, hid = lax.axis_index("grp"), lax.axis_index("seq"), lax.axis_index("hid")
    x, z = hid // 8, grp * 8 + hid % 8
    y, core = seq // 2, seq % 2

    def at(xx, zz, ss):
        return (zz // 8, ss, xx * 8 + zz % 8)

    def each(count, me, fn):
        def step(i, carry):
            fn((me + i) % count)
            return carry
        lax.fori_loop(1, count, step, 0)

    def x_peers(fn):
        each(NX, x, lambda p: fn(p, at(p, z, seq)))

    def s_peers(fn):
        each(NS, seq, lambda p: fn(p, at(x, z, p)))

    def z_distance(i):
        return 8 + (1 - 2 * (i % 2)) * (i // 2)

    def z_peers(fn):
        def step(i, carry):
            p = (z + z_distance(i)) % NZ
            fn(p, at(x, p, seq))
            return carry
        lax.fori_loop(1, NZ, step, 0)

    def xs_peers(fn):
        for dx in (2, 1, 3, 0):
            def step(i, carry):
                p, r = (x + dx) % NX, (seq + i) % NS
                fn(p, at(p, z, r))
                return carry
            lax.fori_loop(1 if dx == 0 else 0, NS, step, 0)

    def rows(i, n):
        return pl.ds(pl.multiple_of(i * n, n), n)

    tile_r, tile_c = rows(z // 4 * 4 + x, 16), rows(z % 4, 256)
    loads = [
        pltpu.make_async_copy(a, b, lsem.at[i])
        for i, (a, b) in enumerate([
            (q_hbm, q), (k_hbm, kt), (vup_hbm, vup.at[x]), (wo_hbm, wo.at[x]), (res_hbm, res),
            (wg_hbm, wg), (wu_hbm, wu), (wd_hbm, wd),
            (freq_hbm, freq_ref), (pos_hbm, pos_ref), (len_hbm, len_ref),
            (new_hbm, new_ref), (gain_hbm, gain_ref),
        ])
    ]
    early = (1, 0, 9, 8, 11, 10)
    for i in early:
        loads[i].start()

    barrier = pltpu.get_barrier_semaphore()

    def greet(p, device):
        pl.semaphore_signal(barrier, inc=1, device_id=device, device_id_type=MESH)

    z_peers(greet)
    xs_peers(greet)

    loads[8].wait()
    loads[9].wait()
    places = (jnp.broadcast_to(pos_ref[...], (8, 128)) + iota((8, 128), 0)).astype(F32)
    angles = places * freq_ref[...]
    cos_table, sin_table = jnp.cos(angles), jnp.sin(angles)
    loads[0].wait()
    rope_in = q[:, LATENT:]
    turn_r, turn_c = iota((ROPE, ROPE), 0), iota((ROPE, ROPE), 1)
    turn = jnp.where(
        turn_c == turn_r + 32, 1.0, jnp.where(turn_c == turn_r - 32, -1.0, 0.0)
    ).astype(BF)
    turned = dot(rope_in, turn)
    cosines = jnp.concatenate([jnp.broadcast_to(cos_table[t:t + 1, :ROPE], (64, ROPE)) for t in range(4)], axis=0)
    sines = jnp.concatenate([jnp.broadcast_to(sin_table[t:t + 1, :ROPE], (64, ROPE)) for t in range(4)], axis=0)
    q_rope = (rope_in.astype(F32) * cosines + turned * sines).astype(BF)
    q_lat = q[:, :LATENT]
    loads[11].wait()
    fresh = new_ref[...].astype(F32)
    fresh = jnp.concatenate([fresh, jnp.zeros((4, LATENT + ROPE), F32)], axis=0)
    fresh_in = fresh[:, LATENT:]
    fresh_turned = dot(fresh_in.astype(BF), turn)
    fresh_rope = fresh_in * cos_table[:, :ROPE] + fresh_turned * sin_table[:, :ROPE]
    new_lat = jnp.concatenate([fresh[:, :LATENT], jnp.zeros((8, LATENT), F32)], axis=0).astype(BF)
    new_rope = jnp.concatenate([fresh_rope, jnp.zeros((8, ROPE), F32)], axis=0).astype(BF)
    near = (dot_t(q_lat, new_lat) + dot_t(q_rope, new_rope)) * score_scale
    loads[1].wait()
    for i in range(13):
        if i not in early:
            loads[i].start()
    loads[10].wait()
    far = (dot(q_lat, kt[:LATENT, :]) + dot(q_rope, kt[LATENT:, :])) * score_scale
    usable = iota((256, 256), 1) + seq * 256 < jnp.broadcast_to(len_ref[...], (256, 256))
    causal = iota((256, 16), 1) + seq * 1024 <= iota((256, 16), 0) // 64
    peak = jnp.maximum(
        jnp.max(jnp.where(usable, far, -1e30), axis=1, keepdims=True),
        jnp.max(jnp.where(causal, near, -1e30), axis=1, keepdims=True),
    )
    peak = jnp.floor(peak * (1.0 / 32.0)) * 32.0
    far_w = jnp.where(usable, jnp.exp(far - peak), 0.0)
    near_w = jnp.where(causal, jnp.exp(near - peak), 0.0)
    total = jnp.sum(far_w, axis=1, keepdims=True) + jnp.sum(near_w, axis=1, keepdims=True)
    mixture = dot_t(far_w.astype(BF), kt[:LATENT, :]) + dot(near_w.astype(BF), new_lat)
    asend[:, :LATENT] = mixture.astype(BF)
    lane = iota((256, 128), 1)
    high = total.astype(BF).astype(F32)
    asend[:, LATENT:] = jnp.where(
        lane == 0, peak, jnp.where(lane == 1, high, total - high)
    ).astype(BF)

    pl.semaphore_wait(barrier, (NX * NS - 1) + (NZ - 1))
    s_peers(lambda p, device: remote(
        asend.at[rows(p, 32)], arecv.at[seq], ssem.at[0], rsem.at[0], device).start())

    half = rows(core, 256)
    x_peers(lambda p, device: remote(
        vup_hbm.at[half], vup.at[x, half], ssem.at[1], rsem.at[1], device).start())
    x_peers(lambda p, device: remote(
        wo_hbm, wo.at[x], ssem.at[2], rsem.at[2], device).start())

    arecv[seq] = asend[rows(seq, 32)]
    perm_one = one_hot(128, 128, lambda o: (o % 4) * 32 + (o // 4 % 4) * 8 + o // 16)
    perm_two = one_hot(256, 256, lambda o: (o % 16) * 16 + o // 16)
    wait_bytes(arecv.at[0:NS - 1], rsem.at[0])

    aux = [arecv[i, :, LATENT:].astype(F32) for i in range(NS)]
    top = functools.reduce(jnp.maximum, [a[:, 0:1] for a in aux])
    factors = [jnp.exp(a[:, 0:1] - top) for a in aux]
    totals = sum(f * (a[:, 1:2] + a[:, 2:3]) for f, a in zip(factors, aux))
    mixed = sum(f * arecv[i, :, :LATENT].astype(F32) for i, f in enumerate(factors))
    heads = (mixed / totals).astype(BF)

    stacked = jnp.concatenate([heads[:, 128 * i:128 * i + 128] for i in range(4)], axis=0)
    zs[...] = dot(perm_one, stacked).astype(BF).reshape(8, 16, 128)

    def to_head(j, carry):
        p = core * 8 + j

        @pl.when(p != z)
        def _():
            remote(zs.at[j], zr.at[z], ssem.at[3], rsem.at[3], at(x, p, seq)).start()

        return carry

    lax.fori_loop(0, 8, to_head, 0)

    other = at(x, z, y * 2 + 1 - core)
    wait_bytes(vup.at[0:NX - 1, 0:256], rsem.at[1])

    def hand_over(p, _):
        piece = vup.at[p, half]
        remote(piece, piece, ssem.at[16], rsem.at[18], other).start()

    x_peers(hand_over)
    loads[2].wait()
    wait_bytes(vup.at[0:NX - 1, 0:256], rsem.at[18])
    value_rows = rows(y, 16)

    @pl.when(grp == core)
    def _():
        zr[z] = zs[z % 8]
        wait_bytes(zr.at[0:NZ - 1], rsem.at[3])
        lat = dot(perm_two, zr[...].reshape(256, 128)).astype(BF)
        for i in range(NX):
            wide = jnp.concatenate([lat[64 * i + 16 * n:64 * i + 16 * n + 16] for n in range(4)], axis=1)
            vbuf[value_rows, 128 * i:128 * i + 128] = dot(wide, vup[i]).astype(BF)
        s_peers(lambda p, device: remote(
            vbuf.at[value_rows], vbuf.at[value_rows], ssem.at[4], rsem.at[4], device).start())

    loads[3].wait()
    wait_bytes(wo.at[0:NX - 1], rsem.at[2])

    @pl.when(grp == core)
    def _():
        wait_bytes(vbuf.at[0:48], rsem.at[4])

    @pl.when(grp != core)
    def _():
        wait_bytes(vbuf, rsem.at[4])

    ob[...] = dot(vbuf[...], wo[...].reshape(512, 1024)).astype(BF)
    z_peers(lambda p, device: remote(
        ob.at[rows(p // 4, 16), rows(p % 4, 256)], orz.at[z], ssem.at[5], rsem.at[5], device).start())
    orz[z] = ob[rows(z // 4, 16), tile_c]
    loads[4].wait()
    loads[12].wait()
    gain = gain_ref[...]
    own = one_hot(16, 256, lambda o: ((o // 8) * 32 + x * 8 + o % 8) * 4 + z // 4)
    old = dot(own, res[:, tile_c])
    wait_bytes(orz.at[0:NZ - 1], rsem.at[5])
    stream = old + sum(orz[i].astype(F32) for i in range(NZ))
    st[...] = stream
    agb[tile_r, tile_c] = (stream * gain_ref[:, tile_c]).astype(BF)
    z_peers(lambda p, device: remote(
        agb.at[tile_r, tile_c], agb.at[tile_r, tile_c], ssem.at[6], fsem.at[z // 4], device).start())

    t_own, side = z // 4, z % 4 // 2
    order = [t_own, (t_own + 3 + 2 * side) % 4, (t_own + 1 + 2 * side) % 4, (t_own + 2) % 4]

    for n, t in enumerate(order):
        piece = agb.at[rows(t * 4 + x, 16)]
        if n == 0:
            wait_bytes(orz.at[0:3], fsem.at[t])
        else:
            wait_bytes(piece, fsem.at[t])
        x_peers(lambda _, device: remote(
            piece, piece, ssem.at[7], rsem.at[16 + n // 2], device).start())

    inverse_gain = 1.0 / gain
    lane = iota((128, 128), 1)
    loads[5].wait()
    loads[6].wait()
    for c in range(2):
        wait_bytes(agb.at[0:96], rsem.at[16 + c])
        scaled = jnp.concatenate([agb[rows(t, 64)] for t in order[2 * c:2 * c + 2]], axis=0)
        gs[c, :, 0:256] = dot(scaled, wg[...]).astype(BF)
        gs[c, :, 256:512] = dot(scaled, wu[...]).astype(BF)
        plain = scaled.astype(F32) * inverse_gain
        squares = jnp.sum(plain * plain, axis=1, keepdims=True)
        high = squares.astype(BF).astype(F32)
        gs[c, :, 512:640] = jnp.where(lane == 0, high, squares - high).astype(BF)
        s_peers(lambda p, device: remote(
            gs.at[c, rows(p, 16)], gr.at[c, seq], ssem.at[8 + c], rsem.at[8 + c], device).start())
        gr[c, seq] = gs[c, rows(seq, 16)]

    mine = rows(seq, 16)
    for c in range(2):
        wait_bytes(gr.at[c, 0:NS - 1], rsem.at[8 + c])
        sums = sum(gr[c, i].astype(F32) for i in range(NS))
        square = sums[:, 512:513] + sums[:, 513:514]
        inverse = lax.rsqrt(square * (1.0 / D) + 1e-06)
        gate = sums[:, 0:256] * inverse
        up = sums[:, 256:512] * inverse
        hb[c, mine] = (gate / (1.0 + jnp.exp(-gate)) * up).astype(BF)
        s_peers(lambda p, device: remote(
            hb.at[c, mine], hb.at[c, mine], ssem.at[10 + c], rsem.at[10 + c], device).start())

    loads[7].wait()
    perm_three = one_hot(256, 256, lambda o: (o % 8) * 32 + (o // 8 % 2) * 16 + o // 16)
    for c in range(2):
        wait_bytes(hb.at[c, 0:112], rsem.at[10 + c])
        ds_[c] = dot(hb[c], wd[...]).astype(BF).reshape(2, 64, 1024)
        if c == 0:
            place = rows(x, 16)
            own = dot(hb[0, place], wd[:, tile_c]) + st[...]
            ds_[0, 0, place, tile_c] = own.astype(BF)
        x_peers(lambda p, device: remote(
            ds_.at[c, :, pl.ds(pl.multiple_of(p * 16, 16), 16)], drx.at[c, x],
            ssem.at[12 + c], rsem.at[12 + c], device).start())
        drx[c, x] = ds_[c, :, pl.ds(pl.multiple_of(x * 16, 16), 16)]

    for c in range(2):
        wait_bytes(drx.at[c, 0:NX - 1], rsem.at[12 + c])
        summed = sum(drx[c, i].astype(F32) for i in range(NX)).astype(BF).reshape(32, 1024)
        stacked = jnp.concatenate([summed[:, 128 * i:128 * i + 128] for i in range(8)], axis=0)
        dz[c] = dot(perm_three, stacked).astype(BF).reshape(NZ, 16, 128)
        z_peers(lambda p, device: remote(
            dz.at[c, p], drz.at[c, z], ssem.at[14 + c], rsem.at[14 + c], device).start())
        drz[c, z] = dz[c, z]

    for c in range(2):
        wait_bytes(drz.at[c, 0:NZ - 1], rsem.at[14 + c])
    final = [0.0] * 4
    for i in range(NZ):
        turn = [i // 4, (i // 4 + 3 + 2 * (i % 4 // 2)) % 4, (i // 4 + 1 + 2 * (i % 4 // 2)) % 4, (i // 4 + 2) % 4]
        for c in range(2):
            part = drz[c, i].astype(F32)
            for n in range(2):
                final[turn[2 * c + n]] += part[8 * n:8 * n + 8]
    for i in range(8):
        out_ref[:, 128 * i:128 * i + 128] = jnp.concatenate([f[i:i + 1] for f in final], axis=0).astype(BF)

    wait_bytes(arecv.at[0:NS - 1], ssem.at[0])
    wait_bytes(vup.at[0:NX - 1, 0:256], ssem.at[1])
    wait_bytes(vup.at[0:NX - 1, 0:256], ssem.at[16])
    wait_bytes(wo.at[0:NX - 1], ssem.at[2])

    @pl.when(grp == core)
    def _():
        wait_bytes(zs.at[0:7], ssem.at[3])
        wait_bytes(wg.at[0:224], ssem.at[4])

    @pl.when(grp != core)
    def _():
        wait_bytes(zs, ssem.at[3])

    wait_bytes(orz.at[0:NZ - 1], ssem.at[5])
    wait_bytes(orz.at[0:NZ - 1], ssem.at[6])
    wait_bytes(agb.at[0:192], ssem.at[7])
    for c in range(2):
        wait_bytes(gr.at[c, 0:NS - 1], ssem.at[8 + c])
        wait_bytes(hb.at[c, 0:112], ssem.at[10 + c])
        wait_bytes(drx.at[c, 0:NX - 1], ssem.at[12 + c])
        wait_bytes(drz.at[c, 0:NZ - 1], ssem.at[14 + c])


def body(
    queries, new_latents, latent_cache, lengths, positions, value_up,
    output_weight, residual, norm_gain, gate_weight, up_weight, down_weight,
):
    halfwidth = ROPE // 2
    frequency = 1000000.0 ** (-np.arange(halfwidth, dtype=np.float64) / halfwidth)
    frequency = jnp.asarray(np.tile(frequency, 4)[None, :], F32)
    vmem, hbm = pl.BlockSpec(memory_space=pltpu.VMEM), pl.BlockSpec(memory_space=pltpu.HBM)

    def buf(*shape, dtype=BF):
        return pltpu.VMEM(shape, dtype)

    return pl.pallas_call(
        kernel,
        out_shape=pltpu.VMEM((4, 1024), BF),
        in_specs=[hbm] * 13,
        out_specs=vmem,
        scratch_shapes=[
            buf(1, 128, dtype=F32), buf(1, 1, dtype=jnp.int32), buf(1, 1, dtype=jnp.int32),
            buf(4, 576), buf(1, 1024, dtype=F32),
            buf(256, 576), buf(576, 256), buf(NX, 512, 128), buf(NX, 128, 1024), buf(256, 1024),
            buf(1024, 256), buf(1024, 256), buf(256, 1024),
            buf(256, 640), buf(NS, 32, 640), buf(8, 16, 128), buf(NZ, 16, 128),
            buf(64, 512), buf(64, 1024), buf(NZ, 16, 256), buf(16, 256, dtype=F32), buf(256, 1024),
            buf(2, 128, 640), buf(2, NS, 16, 640), buf(2, 128, 256),
            buf(2, 2, 64, 1024), buf(2, NX, 2, 16, 1024), buf(2, NZ, 16, 128), buf(2, NZ, 16, 128),
            pltpu.SemaphoreType.DMA((13,)),
            pltpu.SemaphoreType.DMA((17,)),
            pltpu.SemaphoreType.DMA((19,)),
            pltpu.SemaphoreType.DMA((4,)),
        ],
        compiler_params=pltpu.CompilerParams(
            collective_id=0, has_side_effects=True, vmem_limit_bytes=56 * 1024 * 1024,
        ),
        cost_estimate=pl.CostEstimate(flops=10**9, bytes_accessed=4 * 10**6, transcendentals=10**5),
    )(
        frequency, positions.reshape(1, 1), lengths.reshape(1, 1), new_latents.reshape(4, 576), norm_gain.reshape(1, -1),
        queries.reshape(256, 576), jnp.swapaxes(latent_cache.reshape(256, 576), 0, 1), value_up.reshape(512, 128),
        output_weight, residual, gate_weight, up_weight, down_weight,
    )


def solution(mesh):
    rows = ("grp", "hid")
    in_specs = (
        P(rows, None, None, None),
        P(rows, None, None),
        P(rows, "seq", None),
        P(rows),
        P(rows),
        P(rows, None, None),
        P(rows, "seq"),
        P(None, "seq"),
        P("seq"),
        P("seq", rows),
        P("seq", rows),
        P(rows, "seq"),
    )
    return jax.shard_map(body, mesh=mesh, in_specs=in_specs, out_specs=P(rows, "seq"), check_vma=False)
```

```python
import functools

import jax
import jax.numpy as jnp
import numpy as np
from jax import lax
from jax.experimental import pallas as pl
from jax.experimental.pallas import tpu as pltpu
from jax.sharding import PartitionSpec as P

D = 8192
LATENT = 512
ROPE = 64
NX, NZ, NS = 4, 16, 8
MESH = pl.DeviceIdType.MESH
BF = jnp.bfloat16
F32 = jnp.float32
score_scale = 192.0 ** (-0.5)


def dot(a, b):
    return lax.dot_general(a, b, (((1,), (0,)), ((), ())), preferred_element_type=F32)


def dot_t(a, b):
    return lax.dot_general(a, b, (((1,), (1,)), ((), ())), preferred_element_type=F32)


def iota(shape, axis):
    return lax.broadcasted_iota(jnp.int32, shape, axis)


def one_hot(rows, cols, source_of):
    return jnp.where(iota((rows, cols), 1) == source_of(iota((rows, cols), 0)), 1.0, 0.0).astype(BF)


def remote(src, dst, send_sem, recv_sem, device):
    return pltpu.make_async_remote_copy(
        src_ref=src, dst_ref=dst, send_sem=send_sem, recv_sem=recv_sem,
        device_id=device, device_id_type=MESH,
    )


def wait_bytes(ref, sem):
    pltpu.make_async_copy(ref, ref, sem).wait()


def kernel(
    freq_hbm, pos_hbm, len_hbm, new_hbm, gain_hbm,
    q_hbm, k_hbm, vup_hbm, wo_hbm, res_hbm, wg_hbm, wu_hbm, wd_hbm,
    out_ref,
    freq_ref, pos_ref, len_ref, new_ref, gain_ref,
    q, kt, vup, wo, res, wg, wu, wd,
    asend, arecv, zs, zr, vbuf, ob, orz, st, agb, gs, gr, hs, hb, ds_, dz, drz,
    lsem, ssem, rsem, fsem,
):
    grp, seq, hid = lax.axis_index("grp"), lax.axis_index("seq"), lax.axis_index("hid")
    x, z = hid // 8, grp * 8 + hid % 8
    y, core = seq // 2, seq % 2

    def at(xx, zz, ss):
        return (zz // 8, ss, xx * 8 + zz % 8)

    def distance(count, i):
        return count // 2 + (1 - 2 * (i % 2)) * (i // 2)

    def each(count, me, fn):
        def step(i, carry):
            fn((me + distance(count, i)) % count)
            return carry
        lax.fori_loop(1, count, step, 0)

    def x_peers(fn):
        each(NX, x, lambda p: fn(p, at(p, z, seq)))

    def s_peers(fn):
        each(NS, seq, lambda p: fn(p, at(x, z, p)))

    def z_peers(fn):
        each(NZ, z, lambda p: fn(p, at(x, p, seq)))

    def xs_peers(fn):
        for dx in (2, 1, 3, 0):
            def step(i, carry):
                p, r = (x + dx) % NX, (seq + i) % NS
                fn(p, at(p, z, r))
                return carry
            lax.fori_loop(1 if dx == 0 else 0, NS, step, 0)

    def rows(i, n):
        return pl.ds(pl.multiple_of(i * n, n), n)

    tile_r, tile_c = rows(z // 4 * 4 + x, 16), rows(z % 4, 256)
    loads = [
        pltpu.make_async_copy(a, b, lsem.at[i])
        for i, (a, b) in enumerate([
            (q_hbm, q), (k_hbm, kt), (vup_hbm, vup.at[x]), (wo_hbm, wo.at[x]), (res_hbm, res),
            (wg_hbm, wg), (wu_hbm, wu), (wd_hbm, wd.at[x]),
            (freq_hbm, freq_ref), (pos_hbm, pos_ref), (len_hbm, len_ref),
            (new_hbm, new_ref), (gain_hbm, gain_ref),
        ])
    ]
    early = (1, 0, 9, 8, 11, 10)
    for i in early:
        loads[i].start()

    barrier = pltpu.get_barrier_semaphore()

    def greet(p, device):
        pl.semaphore_signal(barrier, inc=1, device_id=device, device_id_type=MESH)

    z_peers(greet)
    xs_peers(greet)

    loads[8].wait()
    loads[9].wait()
    places = (jnp.broadcast_to(pos_ref[...], (8, 128)) + iota((8, 128), 0)).astype(F32)
    angles = places * freq_ref[...]
    cos_table, sin_table = jnp.cos(angles), jnp.sin(angles)
    loads[0].wait()
    rope_in = q[:, LATENT:]
    turn_r, turn_c = iota((ROPE, ROPE), 0), iota((ROPE, ROPE), 1)
    turn = jnp.where(
        turn_c == turn_r + 32, 1.0, jnp.where(turn_c == turn_r - 32, -1.0, 0.0)
    ).astype(BF)
    turned = dot(rope_in, turn)
    cosines = jnp.concatenate([jnp.broadcast_to(cos_table[t:t + 1, :ROPE], (64, ROPE)) for t in range(4)], axis=0)
    sines = jnp.concatenate([jnp.broadcast_to(sin_table[t:t + 1, :ROPE], (64, ROPE)) for t in range(4)], axis=0)
    q_rope = (rope_in.astype(F32) * cosines + turned * sines).astype(BF)
    q_lat = q[:, :LATENT]
    loads[11].wait()
    fresh = new_ref[...].astype(F32)
    fresh = jnp.concatenate([fresh, jnp.zeros((4, LATENT + ROPE), F32)], axis=0)
    fresh_in = fresh[:, LATENT:]
    fresh_turned = dot(fresh_in.astype(BF), turn)
    fresh_rope = fresh_in * cos_table[:, :ROPE] + fresh_turned * sin_table[:, :ROPE]
    new_lat = jnp.concatenate([fresh[:, :LATENT], jnp.zeros((8, LATENT), F32)], axis=0).astype(BF)
    new_rope = jnp.concatenate([fresh_rope, jnp.zeros((8, ROPE), F32)], axis=0).astype(BF)
    near = (dot_t(q_lat, new_lat) + dot_t(q_rope, new_rope)) * score_scale
    loads[1].wait()
    for i in range(13):
        if i not in early:
            loads[i].start()
    loads[10].wait()
    far = (dot(q_lat, kt[:LATENT, :]) + dot(q_rope, kt[LATENT:, :])) * score_scale
    usable = iota((256, 256), 1) + seq * 256 < jnp.broadcast_to(len_ref[...], (256, 256))
    causal = iota((256, 16), 1) + seq * 1024 <= iota((256, 16), 0) // 64
    peak = jnp.maximum(
        jnp.max(jnp.where(usable, far, -1e30), axis=1, keepdims=True),
        jnp.max(jnp.where(causal, near, -1e30), axis=1, keepdims=True),
    )
    peak = jnp.floor(peak * (1.0 / 32.0)) * 32.0
    far_w = jnp.where(usable, jnp.exp(far - peak), 0.0)
    near_w = jnp.where(causal, jnp.exp(near - peak), 0.0)
    total = jnp.sum(far_w, axis=1, keepdims=True) + jnp.sum(near_w, axis=1, keepdims=True)
    mixture = dot_t(far_w.astype(BF), kt[:LATENT, :]) + dot(near_w.astype(BF), new_lat)
    asend[:, :LATENT] = mixture.astype(BF)
    lane = iota((256, 128), 1)
    high = total.astype(BF).astype(F32)
    asend[:, LATENT:] = jnp.where(
        lane == 0, peak, jnp.where(lane == 1, high, total - high)
    ).astype(BF)

    pl.semaphore_wait(barrier, (NX * NS - 1) + (NZ - 1))
    s_peers(lambda p, device: remote(
        asend.at[rows(p, 32)], arecv.at[seq], ssem.at[0], rsem.at[0], device).start())

    half = rows(core, 256)
    x_peers(lambda p, device: remote(
        vup_hbm.at[half], vup.at[x, half], ssem.at[1], rsem.at[1], device).start())
    x_peers(lambda p, device: remote(
        wo_hbm, wo.at[x], ssem.at[2], rsem.at[2], device).start())

    arecv[seq] = asend[rows(seq, 32)]
    perm_one = one_hot(128, 128, lambda o: (o % 4) * 32 + (o // 4 % 4) * 8 + o // 16)
    perm_two = one_hot(256, 256, lambda o: (o % 16) * 16 + o // 16)
    wait_bytes(arecv.at[0:NS - 1], rsem.at[0])

    aux = [arecv[i, :, LATENT:].astype(F32) for i in range(NS)]
    top = functools.reduce(jnp.maximum, [a[:, 0:1] for a in aux])
    factors = [jnp.exp(a[:, 0:1] - top) for a in aux]
    totals = sum(f * (a[:, 1:2] + a[:, 2:3]) for f, a in zip(factors, aux))
    mixed = sum(f * arecv[i, :, :LATENT].astype(F32) for i, f in enumerate(factors))
    heads = (mixed / totals).astype(BF)

    stacked = jnp.concatenate([heads[:, 128 * i:128 * i + 128] for i in range(4)], axis=0)
    zs[...] = dot(perm_one, stacked).astype(BF).reshape(8, 16, 128)

    def to_head(j, carry):
        p = core * 8 + j

        @pl.when(p != z)
        def _():
            remote(zs.at[j], zr.at[z], ssem.at[3], rsem.at[3], at(x, p, seq)).start()

        return carry

    lax.fori_loop(0, 8, to_head, 0)

    left, right = (x + 3) % NX, (x + 1) % NX
    for p, sem in ((right, 12), (left, 19)):
        remote(wd_hbm, wd.at[x], ssem.at[12], rsem.at[sem], at(p, z, seq)).start()

    other = at(x, z, y * 2 + 1 - core)
    wait_bytes(vup.at[0:NX - 1, 0:256], rsem.at[1])

    def hand_over(p, _):
        piece = vup.at[p, half]
        remote(piece, piece, ssem.at[16], rsem.at[18], other).start()

    x_peers(hand_over)
    loads[2].wait()
    wait_bytes(vup.at[0:NX - 1, 0:256], rsem.at[18])
    value_rows = rows(y, 16)

    @pl.when(grp == core)
    def _():
        zr[z] = zs[z % 8]
        wait_bytes(zr.at[0:NZ - 1], rsem.at[3])
        lat = dot(perm_two, zr[...].reshape(256, 128)).astype(BF)
        for i in range(NX):
            wide = jnp.concatenate([lat[64 * i + 16 * n:64 * i + 16 * n + 16] for n in range(4)], axis=1)
            vbuf[value_rows, 128 * i:128 * i + 128] = dot(wide, vup[i]).astype(BF)
        s_peers(lambda p, device: remote(
            vbuf.at[value_rows], vbuf.at[value_rows], ssem.at[4], rsem.at[4], device).start())

    loads[3].wait()
    wait_bytes(wo.at[0:NX - 1], rsem.at[2])

    @pl.when(grp == core)
    def _():
        wait_bytes(vbuf.at[0:48], rsem.at[4])

    @pl.when(grp != core)
    def _():
        wait_bytes(vbuf, rsem.at[4])

    ob[...] = dot(vbuf[...], wo[...].reshape(512, 1024)).astype(BF)
    z_peers(lambda p, device: remote(
        ob.at[rows(p // 4, 16), rows(p % 4, 256)], orz.at[z], ssem.at[5], rsem.at[5], device).start())
    orz[z] = ob[rows(z // 4, 16), tile_c]
    for p, sem, to, part in ((left, 12, right, 0), (right, 19, left, 1)):
        wait_bytes(wd.at[p], rsem.at[sem])
        piece = wd.at[p, 128 * part:128 * part + 128]
        remote(piece, piece, ssem.at[12], rsem.at[20], at(to, z, seq)).start()
    loads[4].wait()
    loads[12].wait()
    gain = gain_ref[...]
    own = one_hot(16, 256, lambda o: ((o // 8) * 32 + x * 8 + o % 8) * 4 + z // 4)
    old = dot(own, res[:, tile_c])
    wait_bytes(orz.at[0:NZ - 1], rsem.at[5])
    stream = old + sum(orz[i].astype(F32) for i in range(NZ))
    st[...] = stream
    agb[tile_r, tile_c] = (stream * gain_ref[:, tile_c]).astype(BF)
    z_peers(lambda p, device: remote(
        agb.at[tile_r, tile_c], agb.at[tile_r, tile_c], ssem.at[6], fsem.at[z // 4], device).start())

    t_own, side = z // 4, z % 4 // 2
    order = [t_own, (t_own + 3 + 2 * side) % 4, (t_own + 1 + 2 * side) % 4, (t_own + 2) % 4]

    for n, t in enumerate(order):
        piece = agb.at[rows(t * 4 + x, 16)]
        if n == 0:
            wait_bytes(orz.at[0:3], fsem.at[t])
        else:
            wait_bytes(piece, fsem.at[t])
        x_peers(lambda _, device: remote(
            piece, piece, ssem.at[7], rsem.at[16 + n // 2], device).start())

    inverse_gain = 1.0 / gain
    lane = iota((128, 128), 1)
    loads[5].wait()
    loads[6].wait()
    for c in range(2):
        wait_bytes(agb.at[0:96], rsem.at[16 + c])
        scaled = jnp.concatenate([agb[rows(t, 64)] for t in order[2 * c:2 * c + 2]], axis=0)
        gs[c, :, 0:256] = dot(scaled, wg[...]).astype(BF)
        gs[c, :, 256:512] = dot(scaled, wu[...]).astype(BF)
        plain = scaled.astype(F32) * inverse_gain
        squares = jnp.sum(plain * plain, axis=1, keepdims=True)
        high = squares.astype(BF).astype(F32)
        gs[c, :, 512:640] = jnp.where(lane == 0, high, squares - high).astype(BF)
        s_peers(lambda p, device: remote(
            gs.at[c, rows(p, 16)], gr.at[c, seq], ssem.at[8 + c], rsem.at[8 + c], device).start())
        gr[c, seq] = gs[c, rows(seq, 16)]

    seq_x, seq_t = seq % 4, seq // 4
    for c in range(2):
        wait_bytes(gr.at[c, 0:NS - 1], rsem.at[8 + c])
        sums = sum(gr[c, i].astype(F32) for i in range(NS))
        square = sums[:, 512:513] + sums[:, 513:514]
        inverse = lax.rsqrt(square * (1.0 / D) + 1e-06)
        gate = sums[:, 0:256] * inverse
        up = sums[:, 256:512] * inverse
        hs[c] = (gate / (1.0 + jnp.exp(-gate)) * up).astype(BF)

        def to_x(p, device):
            place = hb.at[c, rows(seq_t, 16), rows(x, 256)]
            remote(hs.at[c], place, ssem.at[10 + c], rsem.at[10 + c], at(seq_x, z, p)).start()

        s_peers(to_x)

        @pl.when(seq_x != x)
        def _():
            to_x(seq, None)

        @pl.when(seq_x == x)
        def _():
            hb[c, rows(seq_t, 16), rows(x, 256)] = hs[c]

    perm_three = one_hot(512, 512, lambda o: (o % 8) * 64 + (o // 8 % 4) * 16 + o // 32)
    loads[7].wait()
    wait_bytes(wd.at[0], rsem.at[20])
    for c in range(2):
        @pl.when(seq_x == x)
        def _():
            wait_bytes(wg.at[0:112], rsem.at[10 + c])

        @pl.when(seq_x != x)
        def _():
            wait_bytes(wg.at[0:128], rsem.at[10 + c])

    ds_[...] = dot(hb[...].reshape(64, 1024), wd[...].reshape(1024, 1024))
    ds_[0:16, tile_c] = ds_[0:16, tile_c] + st[...]
    stacked = jnp.concatenate([ds_[:, 128 * i:128 * i + 128].astype(BF) for i in range(8)], axis=0)
    dz[...] = dot(perm_three, stacked).astype(BF).reshape(NZ, 32, 128)
    z_peers(lambda p, device: remote(
        dz.at[p], drz.at[z], ssem.at[13], rsem.at[13], device).start())
    drz[z] = dz[z]
    wait_bytes(drz.at[0:NZ - 1], rsem.at[13])
    final = [0.0] * 4
    for i in range(NZ):
        t, side = i // 4, i % 4 // 2
        turn = [t, (t + 3 + 2 * side) % 4, (t + 1 + 2 * side) % 4, (t + 2) % 4]
        part = drz[i].astype(F32)
        for n in range(4):
            final[turn[n]] += part[8 * n:8 * n + 8]
    for i in range(8):
        out_ref[:, 128 * i:128 * i + 128] = jnp.concatenate([f[i:i + 1] for f in final], axis=0).astype(BF)

    wait_bytes(arecv.at[0:NS - 1], ssem.at[0])
    wait_bytes(vup.at[0:NX - 1, 0:256], ssem.at[1])
    wait_bytes(vup.at[0:NX - 1, 0:256], ssem.at[16])
    wait_bytes(wo.at[0:NX - 1], ssem.at[2])

    @pl.when(grp == core)
    def _():
        wait_bytes(zs.at[0:7], ssem.at[3])
        wait_bytes(wg.at[0:224], ssem.at[4])

    @pl.when(grp != core)
    def _():
        wait_bytes(zs, ssem.at[3])

    wait_bytes(orz.at[0:NZ - 1], ssem.at[5])
    wait_bytes(orz.at[0:NZ - 1], ssem.at[6])
    wait_bytes(agb.at[0:192], ssem.at[7])
    for c in range(2):
        wait_bytes(gr.at[c, 0:NS - 1], ssem.at[8 + c])

        @pl.when(seq_x == x)
        def _():
            wait_bytes(wg.at[0:112], ssem.at[10 + c])

        @pl.when(seq_x != x)
        def _():
            wait_bytes(wg.at[0:128], ssem.at[10 + c])

    wait_bytes(wd.at[0:NX - 1], ssem.at[12])
    wait_bytes(drz.at[0:NZ - 1], ssem.at[13])


def body(
    queries, new_latents, latent_cache, lengths, positions, value_up,
    output_weight, residual, norm_gain, gate_weight, up_weight, down_weight,
):
    halfwidth = ROPE // 2
    frequency = 1000000.0 ** (-np.arange(halfwidth, dtype=np.float64) / halfwidth)
    frequency = jnp.asarray(np.tile(frequency, 4)[None, :], F32)
    vmem, hbm = pl.BlockSpec(memory_space=pltpu.VMEM), pl.BlockSpec(memory_space=pltpu.HBM)

    def buf(*shape, dtype=BF):
        return pltpu.VMEM(shape, dtype)

    return pl.pallas_call(
        kernel,
        out_shape=pltpu.VMEM((4, 1024), BF),
        in_specs=[hbm] * 13,
        out_specs=vmem,
        scratch_shapes=[
            buf(1, 128, dtype=F32), buf(1, 1, dtype=jnp.int32), buf(1, 1, dtype=jnp.int32),
            buf(4, 576), buf(1, 1024, dtype=F32),
            buf(256, 576), buf(576, 256), buf(NX, 512, 128), buf(NX, 128, 1024), buf(256, 1024),
            buf(1024, 256), buf(1024, 256), buf(NX, 256, 1024),
            buf(256, 640), buf(NS, 32, 640), buf(8, 16, 128), buf(NZ, 16, 128),
            buf(64, 512), buf(64, 1024), buf(NZ, 16, 256), buf(16, 256, dtype=F32), buf(256, 1024),
            buf(2, 128, 640), buf(2, NS, 16, 640), buf(2, 16, 256), buf(2, 32, 1024),
            buf(64, 1024, dtype=F32), buf(NZ, 32, 128), buf(NZ, 32, 128),
            pltpu.SemaphoreType.DMA((13,)),
            pltpu.SemaphoreType.DMA((17,)),
            pltpu.SemaphoreType.DMA((21,)),
            pltpu.SemaphoreType.DMA((4,)),
        ],
        compiler_params=pltpu.CompilerParams(
            collective_id=0, has_side_effects=True, vmem_limit_bytes=56 * 1024 * 1024,
        ),
        cost_estimate=pl.CostEstimate(flops=10**9, bytes_accessed=4 * 10**6, transcendentals=10**5),
    )(
        frequency, positions.reshape(1, 1), lengths.reshape(1, 1), new_latents.reshape(4, 576), norm_gain.reshape(1, -1),
        queries.reshape(256, 576), jnp.swapaxes(latent_cache.reshape(256, 576), 0, 1), value_up.reshape(512, 128),
        output_weight, residual, gate_weight, up_weight, down_weight,
    )


def solution(mesh):
    rows = ("grp", "hid")
    in_specs = (
        P(rows, None, None, None),
        P(rows, None, None),
        P(rows, "seq", None),
        P(rows),
        P(rows),
        P(rows, None, None),
        P(rows, "seq"),
        P(None, "seq"),
        P("seq"),
        P("seq", rows),
        P("seq", rows),
        P(rows, "seq"),
    )
    return jax.shard_map(body, mesh=mesh, in_specs=in_specs, out_specs=P(rows, "seq"), check_vma=False)
```

```python
import functools

import jax
import jax.numpy as jnp
import numpy as np
from jax import lax
from jax.experimental import pallas as pl
from jax.experimental.pallas import tpu as pltpu
from jax.sharding import PartitionSpec as P

D = 8192
LATENT = 512
ROPE = 64
NX, NZ, NS = 4, 16, 8
MESH = pl.DeviceIdType.MESH
BF = jnp.bfloat16
F32 = jnp.float32
score_scale = 192.0 ** (-0.5)


def dot(a, b):
    return lax.dot_general(a, b, (((1,), (0,)), ((), ())), preferred_element_type=F32)


def dot_t(a, b):
    return lax.dot_general(a, b, (((1,), (1,)), ((), ())), preferred_element_type=F32)


def iota(shape, axis):
    return lax.broadcasted_iota(jnp.int32, shape, axis)


def one_hot(rows, cols, source_of):
    return jnp.where(iota((rows, cols), 1) == source_of(iota((rows, cols), 0)), 1.0, 0.0).astype(BF)


def remote(src, dst, send_sem, recv_sem, device):
    return pltpu.make_async_remote_copy(
        src_ref=src, dst_ref=dst, send_sem=send_sem, recv_sem=recv_sem,
        device_id=device, device_id_type=MESH,
    )


def wait_bytes(ref, sem):
    pltpu.make_async_copy(ref, ref, sem).wait()


def kernel(
    freq_hbm, pos_hbm, len_hbm, new_hbm, gain_hbm,
    q_hbm, k_hbm, vup_hbm, wo_hbm, res_hbm, wg_hbm, wu_hbm, wd_hbm,
    out_ref,
    freq_ref, pos_ref, len_ref, new_ref, gain_ref,
    q, kt, vup, wo, res, wg, wu, wd,
    asend, arecv, zs, zr, vbuf, ob, orz, st, agb, gs, gr, hs, hb, ds_, dz, drz,
    lsem, ssem, rsem, fsem,
):
    grp, seq, hid = lax.axis_index("grp"), lax.axis_index("seq"), lax.axis_index("hid")
    x, z = hid // 8, grp * 8 + hid % 8
    y, core = seq // 2, seq % 2

    def at(xx, zz, ss):
        return (zz // 8, ss, xx * 8 + zz % 8)

    def distance(count, i):
        return count // 2 + (1 - 2 * (i % 2)) * (i // 2)

    def each(count, me, fn):
        def step(i, carry):
            fn((me + distance(count, i)) % count)
            return carry
        lax.fori_loop(1, count, step, 0)

    def x_peers(fn):
        each(NX, x, lambda p: fn(p, at(p, z, seq)))

    def s_peers(fn):
        each(NS, seq, lambda p: fn(p, at(x, z, p)))

    def z_peers(fn):
        each(NZ, z, lambda p: fn(p, at(x, p, seq)))

    def xs_peers(fn):
        for dx in (2, 1, 3, 0):
            def step(i, carry):
                p, r = (x + dx) % NX, (seq + i) % NS
                fn(p, at(p, z, r))
                return carry
            lax.fori_loop(1 if dx == 0 else 0, NS, step, 0)

    def rows(i, n):
        return pl.ds(pl.multiple_of(i * n, n), n)

    tile_r, tile_c = rows(z // 4 * 4 + x, 16), rows(z % 4, 256)
    loads = [
        pltpu.make_async_copy(a, b, lsem.at[i])
        for i, (a, b) in enumerate([
            (q_hbm, q), (k_hbm, kt), (vup_hbm, vup.at[x]), (wo_hbm, wo.at[x]), (res_hbm, res),
            (wg_hbm, wg), (wu_hbm, wu), (wd_hbm, wd.at[x]),
            (freq_hbm, freq_ref), (pos_hbm, pos_ref), (len_hbm, len_ref),
            (new_hbm, new_ref), (gain_hbm, gain_ref),
        ])
    ]
    early = (1, 0, 9, 8, 11, 10)
    for i in early:
        loads[i].start()

    barrier = pltpu.get_barrier_semaphore()

    def greet(p, device):
        pl.semaphore_signal(barrier, inc=1, device_id=device, device_id_type=MESH)

    z_peers(greet)
    xs_peers(greet)

    loads[8].wait()
    loads[9].wait()
    places = (jnp.broadcast_to(pos_ref[...], (8, 128)) + iota((8, 128), 0)).astype(F32)
    angles = places * freq_ref[...]
    cos_table, sin_table = jnp.cos(angles), jnp.sin(angles)
    loads[0].wait()
    rope_in = q[:, LATENT:]
    turn_r, turn_c = iota((ROPE, ROPE), 0), iota((ROPE, ROPE), 1)
    turn = jnp.where(
        turn_c == turn_r + 32, 1.0, jnp.where(turn_c == turn_r - 32, -1.0, 0.0)
    ).astype(BF)
    turned = dot(rope_in, turn)
    cosines = jnp.concatenate([jnp.broadcast_to(cos_table[t:t + 1, :ROPE], (64, ROPE)) for t in range(4)], axis=0)
    sines = jnp.concatenate([jnp.broadcast_to(sin_table[t:t + 1, :ROPE], (64, ROPE)) for t in range(4)], axis=0)
    q_rope = (rope_in.astype(F32) * cosines + turned * sines).astype(BF)
    q_lat = q[:, :LATENT]
    loads[11].wait()
    fresh = new_ref[...].astype(F32)
    fresh = jnp.concatenate([fresh, jnp.zeros((4, LATENT + ROPE), F32)], axis=0)
    fresh_in = fresh[:, LATENT:]
    fresh_turned = dot(fresh_in.astype(BF), turn)
    fresh_rope = fresh_in * cos_table[:, :ROPE] + fresh_turned * sin_table[:, :ROPE]
    new_lat = jnp.concatenate([fresh[:, :LATENT], jnp.zeros((8, LATENT), F32)], axis=0).astype(BF)
    new_rope = jnp.concatenate([fresh_rope, jnp.zeros((8, ROPE), F32)], axis=0).astype(BF)
    near = (dot_t(q_lat, new_lat) + dot_t(q_rope, new_rope)) * score_scale
    loads[1].wait()
    for i in range(13):
        if i not in early:
            loads[i].start()
    loads[10].wait()
    far = (dot(q_lat, kt[:LATENT, :]) + dot(q_rope, kt[LATENT:, :])) * score_scale
    usable = iota((256, 256), 1) + seq * 256 < jnp.broadcast_to(len_ref[...], (256, 256))
    causal = iota((256, 16), 1) + seq * 1024 <= iota((256, 16), 0) // 64
    peak = jnp.maximum(
        jnp.max(jnp.where(usable, far, -1e30), axis=1, keepdims=True),
        jnp.max(jnp.where(causal, near, -1e30), axis=1, keepdims=True),
    )
    peak = jnp.floor(peak * (1.0 / 32.0)) * 32.0
    far_w = jnp.where(usable, jnp.exp(far - peak), 0.0)
    near_w = jnp.where(causal, jnp.exp(near - peak), 0.0)
    total = jnp.sum(far_w, axis=1, keepdims=True) + jnp.sum(near_w, axis=1, keepdims=True)
    mixture = dot_t(far_w.astype(BF), kt[:LATENT, :]) + dot(near_w.astype(BF), new_lat)
    asend[:, :LATENT] = mixture.astype(BF)
    lane = iota((256, 128), 1)
    high = total.astype(BF).astype(F32)
    asend[:, LATENT:] = jnp.where(
        lane == 0, peak, jnp.where(lane == 1, high, total - high)
    ).astype(BF)

    pl.semaphore_wait(barrier, (NX * NS - 1) + (NZ - 1))
    s_peers(lambda p, device: remote(
        asend.at[rows(p, 32)], arecv.at[seq], ssem.at[0], rsem.at[0], device).start())

    half = rows(core, 256)
    x_peers(lambda p, device: remote(
        vup_hbm.at[half], vup.at[x, half], ssem.at[1], rsem.at[1], device).start())
    x_peers(lambda p, device: remote(
        wo_hbm, wo.at[x], ssem.at[2], rsem.at[2], device).start())

    arecv[seq] = asend[rows(seq, 32)]
    perm_one = one_hot(128, 128, lambda o: (o % 4) * 32 + (o // 4 % 4) * 8 + o // 16)
    perm_two = one_hot(256, 256, lambda o: (o % 16) * 16 + o // 16)
    wait_bytes(arecv.at[0:NS - 1], rsem.at[0])

    aux = [arecv[i, :, LATENT:].astype(F32) for i in range(NS)]
    top = functools.reduce(jnp.maximum, [a[:, 0:1] for a in aux])
    factors = [jnp.exp(a[:, 0:1] - top) for a in aux]
    totals = sum(f * (a[:, 1:2] + a[:, 2:3]) for f, a in zip(factors, aux))
    mixed = sum(f * arecv[i, :, :LATENT].astype(F32) for i, f in enumerate(factors))
    heads = (mixed / totals).astype(BF)

    stacked = jnp.concatenate([heads[:, 128 * i:128 * i + 128] for i in range(4)], axis=0)
    zs[...] = dot(perm_one, stacked).astype(BF).reshape(8, 16, 128)

    def to_head(j, carry):
        p = core * 8 + j

        @pl.when(p != z)
        def _():
            remote(zs.at[j], zr.at[z], ssem.at[3], rsem.at[3], at(x, p, seq)).start()

        return carry

    lax.fori_loop(0, 8, to_head, 0)

    left, right = (x + 3) % NX, (x + 1) % NX
    for p, sem in ((right, 12), (left, 19)):
        remote(wd_hbm, wd.at[x], ssem.at[12], rsem.at[sem], at(p, z, seq)).start()

    other = at(x, z, y * 2 + 1 - core)
    wait_bytes(vup.at[0:NX - 1, 0:256], rsem.at[1])

    def hand_over(p, _):
        piece = vup.at[p, half]
        remote(piece, piece, ssem.at[16], rsem.at[18], other).start()

    x_peers(hand_over)
    loads[2].wait()
    wait_bytes(vup.at[0:NX - 1, 0:256], rsem.at[18])
    value_rows = rows(y, 16)

    @pl.when(grp == core)
    def _():
        zr[z] = zs[z % 8]
        wait_bytes(zr.at[0:NZ - 1], rsem.at[3])
        lat = dot(perm_two, zr[...].reshape(256, 128)).astype(BF)
        for i in range(NX):
            wide = jnp.concatenate([lat[64 * i + 16 * n:64 * i + 16 * n + 16] for n in range(4)], axis=1)
            vbuf[value_rows, 128 * i:128 * i + 128] = dot(wide, vup[i]).astype(BF)
        s_peers(lambda p, device: remote(
            vbuf.at[value_rows], vbuf.at[value_rows], ssem.at[4], rsem.at[4], device).start())

    loads[3].wait()
    wait_bytes(wo.at[0:NX - 1], rsem.at[2])

    @pl.when(grp == core)
    def _():
        wait_bytes(vbuf.at[0:48], rsem.at[4])

    @pl.when(grp != core)
    def _():
        wait_bytes(vbuf, rsem.at[4])

    ob[...] = dot(vbuf[...], wo[...].reshape(512, 1024)).astype(BF)
    z_peers(lambda p, device: remote(
        ob.at[rows(p // 4, 16), rows(p % 4, 256)], orz.at[z], ssem.at[5], rsem.at[5], device).start())
    orz[z] = ob[rows(z // 4, 16), tile_c]
    loads[4].wait()
    loads[12].wait()
    gain = gain_ref[...]
    own = one_hot(16, 256, lambda o: ((o // 8) * 32 + x * 8 + o % 8) * 4 + z // 4)
    old = dot(own, res[:, tile_c])
    wait_bytes(orz.at[0:NZ - 1], rsem.at[5])
    stream = old + sum(orz[i].astype(F32) for i in range(NZ))
    st[...] = stream
    agb[tile_r, tile_c] = (stream * gain_ref[:, tile_c]).astype(BF)
    z_peers(lambda p, device: remote(
        agb.at[tile_r, tile_c], agb.at[tile_r, tile_c], ssem.at[6], fsem.at[z // 4], device).start())

    for p, sem, to, part in ((left, 12, right, 0), (right, 19, left, 1)):
        wait_bytes(wd.at[p], rsem.at[sem])
        piece = wd.at[p, 128 * part:128 * part + 128]
        remote(piece, piece, ssem.at[12], rsem.at[20], at(to, z, seq)).start()

    t_own, side = z // 4, z % 4 // 2
    order = [t_own, (t_own + 3 + 2 * side) % 4, (t_own + 1 + 2 * side) % 4, (t_own + 2) % 4]

    for n, t in enumerate(order):
        piece = agb.at[rows(t * 4 + x, 16)]
        if n == 0:
            wait_bytes(orz.at[0:3], fsem.at[t])
        else:
            wait_bytes(piece, fsem.at[t])
        x_peers(lambda _, device: remote(
            piece, piece, ssem.at[7], rsem.at[16 + n // 2], device).start())

    inverse_gain = 1.0 / gain
    lane = iota((128, 128), 1)
    loads[5].wait()
    loads[6].wait()
    for c in range(2):
        wait_bytes(agb.at[0:96], rsem.at[16 + c])
        scaled = jnp.concatenate([agb[rows(t, 64)] for t in order[2 * c:2 * c + 2]], axis=0)
        gs[c, :, 0:256] = dot(scaled, wg[...]).astype(BF)
        gs[c, :, 256:512] = dot(scaled, wu[...]).astype(BF)
        plain = scaled.astype(F32) * inverse_gain
        squares = jnp.sum(plain * plain, axis=1, keepdims=True)
        high = squares.astype(BF).astype(F32)
        gs[c, :, 512:640] = jnp.where(lane == 0, high, squares - high).astype(BF)
        s_peers(lambda p, device: remote(
            gs.at[c, rows(p, 16)], gr.at[c, seq], ssem.at[8 + c], rsem.at[8 + c], device).start())
        gr[c, seq] = gs[c, rows(seq, 16)]

    seq_x, seq_t = seq % 4, seq // 4
    for c in range(2):
        wait_bytes(gr.at[c, 0:NS - 1], rsem.at[8 + c])
        sums = sum(gr[c, i].astype(F32) for i in range(NS))
        square = sums[:, 512:513] + sums[:, 513:514]
        inverse = lax.rsqrt(square * (1.0 / D) + 1e-06)
        gate = sums[:, 0:256] * inverse
        up = sums[:, 256:512] * inverse
        hs[c] = (gate / (1.0 + jnp.exp(-gate)) * up).astype(BF)

        def to_x(p, device):
            place = hb.at[c, rows(seq_t, 16), rows(x, 256)]
            remote(hs.at[c], place, ssem.at[10 + c], rsem.at[10 + c], at(seq_x, z, p)).start()

        s_peers(to_x)

        @pl.when(seq_x != x)
        def _():
            to_x(seq, None)

        @pl.when(seq_x == x)
        def _():
            hb[c, rows(seq_t, 16), rows(x, 256)] = hs[c]

    perm_three = one_hot(512, 512, lambda o: (o % 8) * 64 + (o // 8 % 4) * 16 + o // 32)
    loads[7].wait()
    wait_bytes(wd.at[0], rsem.at[20])
    for c in range(2):
        @pl.when(seq_x == x)
        def _():
            wait_bytes(wg.at[0:112], rsem.at[10 + c])

        @pl.when(seq_x != x)
        def _():
            wait_bytes(wg.at[0:128], rsem.at[10 + c])

    ds_[...] = dot(hb[...].reshape(64, 1024), wd[...].reshape(1024, 1024))
    ds_[0:16, tile_c] = ds_[0:16, tile_c] + st[...]
    stacked = jnp.concatenate([ds_[:, 128 * i:128 * i + 128].astype(BF) for i in range(8)], axis=0)
    dz[...] = dot(perm_three, stacked).astype(BF).reshape(NZ, 32, 128)
    z_peers(lambda p, device: remote(
        dz.at[p], drz.at[z], ssem.at[13], rsem.at[13], device).start())
    drz[z] = dz[z]
    wait_bytes(drz.at[0:NZ - 1], rsem.at[13])
    final = [0.0] * 4
    for i in range(NZ):
        t, side = i // 4, i % 4 // 2
        turn = [t, (t + 3 + 2 * side) % 4, (t + 1 + 2 * side) % 4, (t + 2) % 4]
        part = drz[i].astype(F32)
        for n in range(4):
            final[turn[n]] += part[8 * n:8 * n + 8]
    for i in range(8):
        out_ref[:, 128 * i:128 * i + 128] = jnp.concatenate([f[i:i + 1] for f in final], axis=0).astype(BF)

    wait_bytes(arecv.at[0:NS - 1], ssem.at[0])
    wait_bytes(vup.at[0:NX - 1, 0:256], ssem.at[1])
    wait_bytes(vup.at[0:NX - 1, 0:256], ssem.at[16])
    wait_bytes(wo.at[0:NX - 1], ssem.at[2])

    @pl.when(grp == core)
    def _():
        wait_bytes(zs.at[0:7], ssem.at[3])
        wait_bytes(wg.at[0:224], ssem.at[4])

    @pl.when(grp != core)
    def _():
        wait_bytes(zs, ssem.at[3])

    wait_bytes(orz.at[0:NZ - 1], ssem.at[5])
    wait_bytes(orz.at[0:NZ - 1], ssem.at[6])
    wait_bytes(agb.at[0:192], ssem.at[7])
    for c in range(2):
        wait_bytes(gr.at[c, 0:NS - 1], ssem.at[8 + c])

        @pl.when(seq_x == x)
        def _():
            wait_bytes(wg.at[0:112], ssem.at[10 + c])

        @pl.when(seq_x != x)
        def _():
            wait_bytes(wg.at[0:128], ssem.at[10 + c])

    wait_bytes(wd.at[0:NX - 1], ssem.at[12])
    wait_bytes(drz.at[0:NZ - 1], ssem.at[13])


def body(
    queries, new_latents, latent_cache, lengths, positions, value_up,
    output_weight, residual, norm_gain, gate_weight, up_weight, down_weight,
):
    halfwidth = ROPE // 2
    frequency = 1000000.0 ** (-np.arange(halfwidth, dtype=np.float64) / halfwidth)
    frequency = jnp.asarray(np.tile(frequency, 4)[None, :], F32)
    vmem, hbm = pl.BlockSpec(memory_space=pltpu.VMEM), pl.BlockSpec(memory_space=pltpu.HBM)

    def buf(*shape, dtype=BF):
        return pltpu.VMEM(shape, dtype)

    return pl.pallas_call(
        kernel,
        out_shape=pltpu.VMEM((4, 1024), BF),
        in_specs=[hbm] * 13,
        out_specs=vmem,
        scratch_shapes=[
            buf(1, 128, dtype=F32), buf(1, 1, dtype=jnp.int32), buf(1, 1, dtype=jnp.int32),
            buf(4, 576), buf(1, 1024, dtype=F32),
            buf(256, 576), buf(576, 256), buf(NX, 512, 128), buf(NX, 128, 1024), buf(256, 1024),
            buf(1024, 256), buf(1024, 256), buf(NX, 256, 1024),
            buf(256, 640), buf(NS, 32, 640), buf(8, 16, 128), buf(NZ, 16, 128),
            buf(64, 512), buf(64, 1024), buf(NZ, 16, 256), buf(16, 256, dtype=F32), buf(256, 1024),
            buf(2, 128, 640), buf(2, NS, 16, 640), buf(2, 16, 256), buf(2, 32, 1024),
            buf(64, 1024, dtype=F32), buf(NZ, 32, 128), buf(NZ, 32, 128),
            pltpu.SemaphoreType.DMA((13,)),
            pltpu.SemaphoreType.DMA((17,)),
            pltpu.SemaphoreType.DMA((21,)),
            pltpu.SemaphoreType.DMA((4,)),
        ],
        compiler_params=pltpu.CompilerParams(
            collective_id=0, has_side_effects=True, vmem_limit_bytes=56 * 1024 * 1024,
        ),
        cost_estimate=pl.CostEstimate(flops=10**9, bytes_accessed=4 * 10**6, transcendentals=10**5),
    )(
        frequency, positions.reshape(1, 1), lengths.reshape(1, 1), new_latents.reshape(4, 576), norm_gain.reshape(1, -1),
        queries.reshape(256, 576), jnp.swapaxes(latent_cache.reshape(256, 576), 0, 1), value_up.reshape(512, 128),
        output_weight, residual, gate_weight, up_weight, down_weight,
    )


def solution(mesh):
    rows = ("grp", "hid")
    in_specs = (
        P(rows, None, None, None),
        P(rows, None, None),
        P(rows, "seq", None),
        P(rows),
        P(rows),
        P(rows, None, None),
        P(rows, "seq"),
        P(None, "seq"),
        P("seq"),
        P("seq", rows),
        P("seq", rows),
        P(rows, "seq"),
    )
    return jax.shard_map(body, mesh=mesh, in_specs=in_specs, out_specs=P(rows, "seq"), check_vma=False)
```

```python
import functools

import jax
import jax.numpy as jnp
import numpy as np
from jax import lax
from jax.experimental import pallas as pl
from jax.experimental.pallas import tpu as pltpu
from jax.sharding import PartitionSpec as P

D = 8192
LATENT = 512
ROPE = 64
NX, NZ, NS = 4, 16, 8
MESH = pl.DeviceIdType.MESH
BF = jnp.bfloat16
F32 = jnp.float32
score_scale = 192.0 ** (-0.5)


def dot(a, b):
    return lax.dot_general(a, b, (((1,), (0,)), ((), ())), preferred_element_type=F32)


def dot_t(a, b):
    return lax.dot_general(a, b, (((1,), (1,)), ((), ())), preferred_element_type=F32)


def iota(shape, axis):
    return lax.broadcasted_iota(jnp.int32, shape, axis)


def one_hot(rows, cols, source_of):
    return jnp.where(iota((rows, cols), 1) == source_of(iota((rows, cols), 0)), 1.0, 0.0).astype(BF)


def remote(src, dst, send_sem, recv_sem, device):
    return pltpu.make_async_remote_copy(
        src_ref=src, dst_ref=dst, send_sem=send_sem, recv_sem=recv_sem,
        device_id=device, device_id_type=MESH,
    )


def wait_bytes(ref, sem):
    pltpu.make_async_copy(ref, ref, sem).wait()


def kernel(
    freq_hbm, pos_hbm, len_hbm, new_hbm, gain_hbm,
    q_hbm, k_hbm, vup_hbm, wo_hbm, res_hbm, wg_hbm, wu_hbm, wd_hbm,
    out_ref,
    freq_ref, pos_ref, len_ref, new_ref, gain_ref,
    q, kt, vup, wo, res, wg, wu, wd,
    asend, arecv, zs, zr, vbuf, ob, orz, st, agb, gs, gr, hs, hb, ds_, dz, drz,
    lsem, ssem, rsem, fsem,
):
    grp, seq, hid = lax.axis_index("grp"), lax.axis_index("seq"), lax.axis_index("hid")
    x, z = hid // 8, grp * 8 + hid % 8
    y, core = seq // 2, seq % 2

    def at(xx, zz, ss):
        return (zz // 8, ss, xx * 8 + zz % 8)

    def distance(count, i):
        return count // 2 + (1 - 2 * (i % 2)) * (i // 2)

    def each(count, me, fn):
        def step(i, carry):
            fn((me + distance(count, i)) % count)
            return carry
        lax.fori_loop(1, count, step, 0)

    def x_peers(fn):
        each(NX, x, lambda p: fn(p, at(p, z, seq)))

    def s_peers(fn):
        each(NS, seq, lambda p: fn(p, at(x, z, p)))

    def z_peers(fn):
        each(NZ, z, lambda p: fn(p, at(x, p, seq)))

    def xs_peers(fn):
        for dx in (2, 1, 3, 0):
            def step(i, carry):
                p, r = (x + dx) % NX, (seq + i) % NS
                fn(p, at(p, z, r))
                return carry
            lax.fori_loop(1 if dx == 0 else 0, NS, step, 0)

    def rows(i, n):
        return pl.ds(pl.multiple_of(i * n, n), n)

    tile_r, tile_c = rows(z // 4 * 4 + x, 16), rows(z % 4, 256)
    loads = [
        pltpu.make_async_copy(a, b, lsem.at[i])
        for i, (a, b) in enumerate([
            (q_hbm, q), (k_hbm, kt), (vup_hbm, vup.at[x]), (wo_hbm, wo.at[x]), (res_hbm, res),
            (wg_hbm, wg), (wu_hbm, wu), (wd_hbm, wd.at[x]),
            (freq_hbm, freq_ref), (pos_hbm, pos_ref), (len_hbm, len_ref),
            (new_hbm, new_ref), (gain_hbm, gain_ref),
        ])
    ]
    early = (1, 0, 9, 8, 11, 10)
    for i in early:
        loads[i].start()

    barrier = pltpu.get_barrier_semaphore()

    def greet(p, device):
        pl.semaphore_signal(barrier, inc=1, device_id=device, device_id_type=MESH)

    z_peers(greet)
    xs_peers(greet)

    loads[8].wait()
    loads[9].wait()
    places = (jnp.broadcast_to(pos_ref[...], (8, 128)) + iota((8, 128), 0)).astype(F32)
    angles = places * freq_ref[...]
    cos_table, sin_table = jnp.cos(angles), jnp.sin(angles)
    loads[0].wait()
    rope_in = q[:, LATENT:]
    turn_r, turn_c = iota((ROPE, ROPE), 0), iota((ROPE, ROPE), 1)
    turn = jnp.where(
        turn_c == turn_r + 32, 1.0, jnp.where(turn_c == turn_r - 32, -1.0, 0.0)
    ).astype(BF)
    turned = dot(rope_in, turn)
    cosines = jnp.concatenate([jnp.broadcast_to(cos_table[t:t + 1, :ROPE], (64, ROPE)) for t in range(4)], axis=0)
    sines = jnp.concatenate([jnp.broadcast_to(sin_table[t:t + 1, :ROPE], (64, ROPE)) for t in range(4)], axis=0)
    q_rope = (rope_in.astype(F32) * cosines + turned * sines).astype(BF)
    q_lat = q[:, :LATENT]
    loads[11].wait()
    fresh = new_ref[...].astype(F32)
    fresh = jnp.concatenate([fresh, jnp.zeros((4, LATENT + ROPE), F32)], axis=0)
    fresh_in = fresh[:, LATENT:]
    fresh_turned = dot(fresh_in.astype(BF), turn)
    fresh_rope = fresh_in * cos_table[:, :ROPE] + fresh_turned * sin_table[:, :ROPE]
    new_lat = jnp.concatenate([fresh[:, :LATENT], jnp.zeros((8, LATENT), F32)], axis=0).astype(BF)
    new_rope = jnp.concatenate([fresh_rope, jnp.zeros((8, ROPE), F32)], axis=0).astype(BF)
    near = (dot_t(q_lat, new_lat) + dot_t(q_rope, new_rope)) * score_scale
    loads[1].wait()
    for i in range(13):
        if i not in early:
            loads[i].start()
    loads[10].wait()
    far = (dot(q_lat, kt[:LATENT, :]) + dot(q_rope, kt[LATENT:, :])) * score_scale
    usable = iota((256, 256), 1) + seq * 256 < jnp.broadcast_to(len_ref[...], (256, 256))
    causal = iota((256, 16), 1) + seq * 1024 <= iota((256, 16), 0) // 64
    peak = jnp.maximum(
        jnp.max(jnp.where(usable, far, -1e30), axis=1, keepdims=True),
        jnp.max(jnp.where(causal, near, -1e30), axis=1, keepdims=True),
    )
    peak = jnp.floor(peak * (1.0 / 32.0)) * 32.0
    far_w = jnp.where(usable, jnp.exp(far - peak), 0.0)
    near_w = jnp.where(causal, jnp.exp(near - peak), 0.0)
    total = jnp.sum(far_w, axis=1, keepdims=True) + jnp.sum(near_w, axis=1, keepdims=True)
    mixture = dot_t(far_w.astype(BF), kt[:LATENT, :]) + dot(near_w.astype(BF), new_lat)
    asend[:, :LATENT] = mixture.astype(BF)
    lane = iota((256, 128), 1)
    high = total.astype(BF).astype(F32)
    asend[:, LATENT:] = jnp.where(
        lane == 0, peak, jnp.where(lane == 1, high, total - high)
    ).astype(BF)

    pl.semaphore_wait(barrier, (NX * NS - 1) + (NZ - 1))
    s_peers(lambda p, device: remote(
        asend.at[rows(p, 32)], arecv.at[seq], ssem.at[0], rsem.at[0], device).start())

    half = rows(core, 256)
    x_peers(lambda p, device: remote(
        vup_hbm.at[half], vup.at[x, half], ssem.at[1], rsem.at[1], device).start())
    x_peers(lambda p, device: remote(
        wo_hbm, wo.at[x], ssem.at[2], rsem.at[2], device).start())

    arecv[seq] = asend[rows(seq, 32)]
    perm_one = one_hot(128, 128, lambda o: (o % 4) * 32 + (o // 4 % 4) * 8 + o // 16)
    perm_two = one_hot(256, 256, lambda o: (o % 16) * 16 + o // 16)
    wait_bytes(arecv.at[0:NS - 1], rsem.at[0])

    aux = [arecv[i, :, LATENT:].astype(F32) for i in range(NS)]
    top = functools.reduce(jnp.maximum, [a[:, 0:1] for a in aux])
    factors = [jnp.exp(a[:, 0:1] - top) for a in aux]
    totals = sum(f * (a[:, 1:2] + a[:, 2:3]) for f, a in zip(factors, aux))
    mixed = sum(f * arecv[i, :, :LATENT].astype(F32) for i, f in enumerate(factors))
    heads = (mixed / totals).astype(BF)

    stacked = jnp.concatenate([heads[:, 128 * i:128 * i + 128] for i in range(4)], axis=0)
    zs[...] = dot(perm_one, stacked).astype(BF).reshape(8, 16, 128)

    def to_head(j, carry):
        p = core * 8 + j

        @pl.when(p != z)
        def _():
            remote(zs.at[j], zr.at[z], ssem.at[3], rsem.at[3], at(x, p, seq)).start()

        return carry

    lax.fori_loop(0, 8, to_head, 0)

    left, right = (x + 3) % NX, (x + 1) % NX
    for p, sem in ((right, 12), (left, 19)):
        remote(wd_hbm, wd.at[x], ssem.at[12], rsem.at[sem], at(p, z, seq)).start()

    other = at(x, z, y * 2 + 1 - core)
    wait_bytes(vup.at[0:NX - 1, 0:256], rsem.at[1])

    def hand_over(p, _):
        piece = vup.at[p, half]
        remote(piece, piece, ssem.at[16], rsem.at[18], other).start()

    x_peers(hand_over)
    loads[2].wait()
    wait_bytes(vup.at[0:NX - 1, 0:256], rsem.at[18])
    value_rows = rows(y, 16)

    @pl.when(grp == core)
    def _():
        zr[z] = zs[z % 8]
        wait_bytes(zr.at[0:NZ - 1], rsem.at[3])
        lat = dot(perm_two, zr[...].reshape(256, 128)).astype(BF)
        for i in range(NX):
            wide = jnp.concatenate([lat[64 * i + 16 * n:64 * i + 16 * n + 16] for n in range(4)], axis=1)
            vbuf[value_rows, 128 * i:128 * i + 128] = dot(wide, vup[i]).astype(BF)
        s_peers(lambda p, device: remote(
            vbuf.at[value_rows], vbuf.at[value_rows], ssem.at[4], rsem.at[4], device).start())

    loads[3].wait()
    wait_bytes(wo.at[0:NX - 1], rsem.at[2])

    @pl.when(grp == core)
    def _():
        wait_bytes(vbuf.at[0:48], rsem.at[4])

    @pl.when(grp != core)
    def _():
        wait_bytes(vbuf, rsem.at[4])

    ob[...] = dot(vbuf[...], wo[...].reshape(512, 1024)).astype(BF)
    z_peers(lambda p, device: remote(
        ob.at[rows(p // 4, 16), rows(p % 4, 256)], orz.at[z], ssem.at[5], rsem.at[5], device).start())
    orz[z] = ob[rows(z // 4, 16), tile_c]
    loads[4].wait()
    loads[12].wait()
    gain = gain_ref[...]
    own = one_hot(16, 256, lambda o: ((o // 8) * 32 + x * 8 + o % 8) * 4 + z // 4)
    old = dot(own, res[:, tile_c])
    wait_bytes(orz.at[0:NZ - 1], rsem.at[5])
    stream = old + sum(orz[i].astype(F32) for i in range(NZ))
    st[...] = stream
    agb[tile_r, tile_c] = (stream * gain_ref[:, tile_c]).astype(BF)
    z_peers(lambda p, device: remote(
        agb.at[tile_r, tile_c], agb.at[tile_r, tile_c], ssem.at[6], fsem.at[z // 4], device).start())

    t_own, side = z // 4, z % 4 // 2
    order = [t_own, (t_own + 3 + 2 * side) % 4, (t_own + 1 + 2 * side) % 4, (t_own + 2) % 4]

    for n, t in enumerate(order):
        piece = agb.at[rows(t * 4 + x, 16)]
        if n == 0:
            wait_bytes(orz.at[0:3], fsem.at[t])
        else:
            wait_bytes(piece, fsem.at[t])
        x_peers(lambda _, device: remote(
            piece, piece, ssem.at[7], rsem.at[16 + n // 2], device).start())

    for p, sem, to, part in ((left, 12, right, 0), (right, 19, left, 1)):
        wait_bytes(wd.at[p], rsem.at[sem])
        piece = wd.at[p, 128 * part:128 * part + 128]
        remote(piece, piece, ssem.at[12], rsem.at[20], at(to, z, seq)).start()

    inverse_gain = 1.0 / gain
    lane = iota((128, 128), 1)
    loads[5].wait()
    loads[6].wait()
    for c in range(2):
        wait_bytes(agb.at[0:96], rsem.at[16 + c])
        scaled = jnp.concatenate([agb[rows(t, 64)] for t in order[2 * c:2 * c + 2]], axis=0)
        gs[c, :, 0:256] = dot(scaled, wg[...]).astype(BF)
        gs[c, :, 256:512] = dot(scaled, wu[...]).astype(BF)
        plain = scaled.astype(F32) * inverse_gain
        squares = jnp.sum(plain * plain, axis=1, keepdims=True)
        high = squares.astype(BF).astype(F32)
        gs[c, :, 512:640] = jnp.where(lane == 0, high, squares - high).astype(BF)
        s_peers(lambda p, device: remote(
            gs.at[c, rows(p, 16)], gr.at[c, seq], ssem.at[8 + c], rsem.at[8 + c], device).start())
        gr[c, seq] = gs[c, rows(seq, 16)]

    seq_x, seq_t = seq % 4, seq // 4
    for c in range(2):
        wait_bytes(gr.at[c, 0:NS - 1], rsem.at[8 + c])
        sums = sum(gr[c, i].astype(F32) for i in range(NS))
        square = sums[:, 512:513] + sums[:, 513:514]
        inverse = lax.rsqrt(square * (1.0 / D) + 1e-06)
        gate = sums[:, 0:256] * inverse
        up = sums[:, 256:512] * inverse
        hs[c] = (gate / (1.0 + jnp.exp(-gate)) * up).astype(BF)

        def to_x(p, device):
            place = hb.at[c, rows(seq_t, 16), rows(x, 256)]
            remote(hs.at[c], place, ssem.at[10 + c], rsem.at[10 + c], at(seq_x, z, p)).start()

        s_peers(to_x)

        @pl.when(seq_x != x)
        def _():
            to_x(seq, None)

        @pl.when(seq_x == x)
        def _():
            hb[c, rows(seq_t, 16), rows(x, 256)] = hs[c]

    perm_three = one_hot(512, 512, lambda o: (o % 8) * 64 + (o // 8 % 4) * 16 + o // 32)
    loads[7].wait()
    wait_bytes(wd.at[0], rsem.at[20])
    for c in range(2):
        @pl.when(seq_x == x)
        def _():
            wait_bytes(wg.at[0:112], rsem.at[10 + c])

        @pl.when(seq_x != x)
        def _():
            wait_bytes(wg.at[0:128], rsem.at[10 + c])

    ds_[...] = dot(hb[...].reshape(64, 1024), wd[...].reshape(1024, 1024))
    ds_[0:16, tile_c] = ds_[0:16, tile_c] + st[...]
    stacked = jnp.concatenate([ds_[:, 128 * i:128 * i + 128].astype(BF) for i in range(8)], axis=0)
    dz[...] = dot(perm_three, stacked).astype(BF).reshape(NZ, 32, 128)
    z_peers(lambda p, device: remote(
        dz.at[p], drz.at[z], ssem.at[13], rsem.at[13], device).start())
    drz[z] = dz[z]
    wait_bytes(drz.at[0:NZ - 1], rsem.at[13])
    final = [0.0] * 4
    for i in range(NZ):
        t, side = i // 4, i % 4 // 2
        turn = [t, (t + 3 + 2 * side) % 4, (t + 1 + 2 * side) % 4, (t + 2) % 4]
        part = drz[i].astype(F32)
        for n in range(4):
            final[turn[n]] += part[8 * n:8 * n + 8]
    for i in range(8):
        out_ref[:, 128 * i:128 * i + 128] = jnp.concatenate([f[i:i + 1] for f in final], axis=0).astype(BF)

    wait_bytes(arecv.at[0:NS - 1], ssem.at[0])
    wait_bytes(vup.at[0:NX - 1, 0:256], ssem.at[1])
    wait_bytes(vup.at[0:NX - 1, 0:256], ssem.at[16])
    wait_bytes(wo.at[0:NX - 1], ssem.at[2])

    @pl.when(grp == core)
    def _():
        wait_bytes(zs.at[0:7], ssem.at[3])
        wait_bytes(wg.at[0:224], ssem.at[4])

    @pl.when(grp != core)
    def _():
        wait_bytes(zs, ssem.at[3])

    wait_bytes(orz.at[0:NZ - 1], ssem.at[5])
    wait_bytes(orz.at[0:NZ - 1], ssem.at[6])
    wait_bytes(agb.at[0:192], ssem.at[7])
    for c in range(2):
        wait_bytes(gr.at[c, 0:NS - 1], ssem.at[8 + c])

        @pl.when(seq_x == x)
        def _():
            wait_bytes(wg.at[0:112], ssem.at[10 + c])

        @pl.when(seq_x != x)
        def _():
            wait_bytes(wg.at[0:128], ssem.at[10 + c])

    wait_bytes(wd.at[0:NX - 1], ssem.at[12])
    wait_bytes(drz.at[0:NZ - 1], ssem.at[13])


def body(
    queries, new_latents, latent_cache, lengths, positions, value_up,
    output_weight, residual, norm_gain, gate_weight, up_weight, down_weight,
):
    halfwidth = ROPE // 2
    frequency = 1000000.0 ** (-np.arange(halfwidth, dtype=np.float64) / halfwidth)
    frequency = jnp.asarray(np.tile(frequency, 4)[None, :], F32)
    vmem, hbm = pl.BlockSpec(memory_space=pltpu.VMEM), pl.BlockSpec(memory_space=pltpu.HBM)

    def buf(*shape, dtype=BF):
        return pltpu.VMEM(shape, dtype)

    return pl.pallas_call(
        kernel,
        out_shape=pltpu.VMEM((4, 1024), BF),
        in_specs=[hbm] * 13,
        out_specs=vmem,
        scratch_shapes=[
            buf(1, 128, dtype=F32), buf(1, 1, dtype=jnp.int32), buf(1, 1, dtype=jnp.int32),
            buf(4, 576), buf(1, 1024, dtype=F32),
            buf(256, 576), buf(576, 256), buf(NX, 512, 128), buf(NX, 128, 1024), buf(256, 1024),
            buf(1024, 256), buf(1024, 256), buf(NX, 256, 1024),
            buf(256, 640), buf(NS, 32, 640), buf(8, 16, 128), buf(NZ, 16, 128),
            buf(64, 512), buf(64, 1024), buf(NZ, 16, 256), buf(16, 256, dtype=F32), buf(256, 1024),
            buf(2, 128, 640), buf(2, NS, 16, 640), buf(2, 16, 256), buf(2, 32, 1024),
            buf(64, 1024, dtype=F32), buf(NZ, 32, 128), buf(NZ, 32, 128),
            pltpu.SemaphoreType.DMA((13,)),
            pltpu.SemaphoreType.DMA((17,)),
            pltpu.SemaphoreType.DMA((21,)),
            pltpu.SemaphoreType.DMA((4,)),
        ],
        compiler_params=pltpu.CompilerParams(
            collective_id=0, has_side_effects=True, vmem_limit_bytes=56 * 1024 * 1024,
        ),
        cost_estimate=pl.CostEstimate(flops=10**9, bytes_accessed=4 * 10**6, transcendentals=10**5),
    )(
        frequency, positions.reshape(1, 1), lengths.reshape(1, 1), new_latents.reshape(4, 576), norm_gain.reshape(1, -1),
        queries.reshape(256, 576), jnp.swapaxes(latent_cache.reshape(256, 576), 0, 1), value_up.reshape(512, 128),
        output_weight, residual, gate_weight, up_weight, down_weight,
    )


def solution(mesh):
    rows = ("grp", "hid")
    in_specs = (
        P(rows, None, None, None),
        P(rows, None, None),
        P(rows, "seq", None),
        P(rows),
        P(rows),
        P(rows, None, None),
        P(rows, "seq"),
        P(None, "seq"),
        P("seq"),
        P("seq", rows),
        P("seq", rows),
        P(rows, "seq"),
    )
    return jax.shard_map(body, mesh=mesh, in_specs=in_specs, out_specs=P(rows, "seq"), check_vma=False)
```
